32 devices in a mesh: head: 4 (over x, core), seq: 8 (over z, y).
Axes of the slice: x: 2, y: 2, z: 4, core: 2. Of those that a mesh axis runs over, the one named last changes fastest.
Arguments:
- tokens: bfloat16 [4096, 4, 768], P('seq'), may hold values from -6 to 6
- attn_gain: float32 [768], replicated, may hold values from 0.5 to 1.5
- qkv_weight: bfloat16 [768, 2304], P(None, 'head'), may hold values from -0.21875 to 0.21875
- bias_table: float32 [32, 12], P(None, 'head'), may hold values from -4 to 4
- proj_weight: bfloat16 [768, 768], P('head'), may hold values from -6 to 6
- ffn_gain: float32 [768], replicated, may hold values from 0.5 to 1.5
- router_weight: bfloat16 [768, 32], replicated, may hold values from -0.15625 to 0.15625
- router_bias: float32 [32], replicated, may hold values from -3 to 3
- expert_in: bfloat16 [32, 768, 3072], P(('head', 'seq')), may hold values from -0.21875 to 0.21875
- expert_out: bfloat16 [32, 3072, 768], P(('head', 'seq')), may hold values from -6 to 6
- bucket: int32 [8192], replicated, may hold values from 0 to 31
- expert_choice: int32 [4096, 4], P('seq', 'head'), may hold values from 0 to 31
- priority: int32 [4096, 4], P('seq', 'head'), may hold values from 0 to 16383, as said below
- out_grad: bfloat16 [4096, 4, 768], P('seq', 'head'), may hold values from -6 to 6
Outputs:
- output: bfloat16 [4096, 4, 768], P('seq', 'head')
- grad_tokens: bfloat16 [4096, 4, 768], P('seq', 'head')
- grad_attn_gain: float32 [768], replicated
- grad_qkv_weight: float32 [768, 2304], P(None, 'head')
- grad_bias_table: float32 [32, 12], P(None, 'head')
- grad_proj_weight: float32 [768, 768], P('head')
- grad_ffn_gain: float32 [768], replicated
- grad_router_weight: float32 [768, 32], replicated
- grad_router_bias: float32 [32], replicated
- grad_expert_in: float32 [32, 768, 3072], P(('head', 'seq'))
- grad_expert_out: float32 [32, 3072, 768], P(('head', 'seq'))
The draws below stay inside these ranges and needn't reach their ends.
Inputs may be any that keep to these rules, and one draw needn't show every extreme that they name: `priority`: each number occurs once.
All inputs are finite; a program needn't handle non-finite values.
Results may differ from the reference program's by a relative error of at most 0.019.
Values may be sent and summed in bfloat16 or wider, within the bound.
A program may use at most 1.3125 GiB of HBM per device.

```python
import jax
import jax.numpy as jnp
from jax import lax

D = 768
HEADS = 12
HEAD_DIM = 64
FF = 3072
NB = 32
SEQS = 4
LEN = 4096
TSD = 512
SB = 1
ROWS_MOE = 512
EXPERTS = 32
CAP = 20
N_HEAD = 4
N_SEQ = 8
DEVICES = 32


def draw_expert_choice(key, part):
    key = jax.random.fold_in(key, 11)
    first, second, third, fourth = jax.random.split(key, 4)
    shape = (LEN, SEQS)
    picks = jnp.minimum(jax.random.randint(first, shape, 0, EXPERTS), jax.random.randint(second, shape, 0, EXPERTS))
    ranking = jax.random.permutation(third, EXPERTS).astype(jnp.int32)
    chosen = ranking[picks]
    offset = jax.random.randint(fourth, (), 0, ROWS_MOE - CAP - 1)
    position = jnp.arange(LEN, dtype=jnp.int32)
    sequence = jnp.arange(SEQS, dtype=jnp.int32)
    flat = (position % TSD)[:, None] * SB + (sequence % SB)[None, :]
    block = (sequence // SB)[None, :] * (LEN // TSD) + (position // TSD)[:, None]
    crowded = (flat >= offset) & (flat < offset + CAP + 1)
    cover = flat == (offset + CAP + 1) % ROWS_MOE
    chosen = jnp.where(cover, ranking[block % EXPERTS], chosen)
    return jnp.where(crowded, ranking[0], chosen).astype(jnp.int32)


def draw_priority(key, part):
    key = jax.random.fold_in(key, 23)
    return jax.random.permutation(key, LEN * SEQS).reshape(LEN, SEQS).astype(jnp.int32)


def set_ends(array, rng, smallest, top_value):
    dims = array.shape
    index_at = [jax.random.randint(jax.random.fold_in(rng, axis), (), 0, dims[axis]) for axis in range(len(dims))]
    array = array.at[tuple(index_at)].set(smallest)
    longest = dims.index(max(dims))
    index_at[longest] = (index_at[longest] + 1) % dims[longest]
    return array.at[tuple(index_at)].set(top_value)


def steps_of(key, shape, cuts, least, largest):
    loudness = 1.0
    for axis_at, parts in cuts:
        draws = jax.random.uniform(jax.random.fold_in(jax.random.fold_in(key, 6), axis_at), (parts,), jnp.float32, least / len(cuts), largest / len(cuts))
        loudness = loudness * jnp.repeat(jnp.exp(draws), shape[axis_at] // parts).reshape((-1,) + (1,) * (len(shape) - 1 - axis_at))
    return loudness


def scatter_about(own_key, shape, width, limit, shards=(), held_as=jnp.bfloat16):
    factor_of = steps_of(own_key, shape, shards, -0.22, 0.18) if shards else 1.0
    entries = jax.random.normal(own_key, shape, jnp.float32) * width * factor_of
    return jnp.minimum(jnp.maximum(entries, -limit), limit).astype(held_as)


def setup_inputs(seed: int = 0) -> dict:
    splits = jax.random.split(jax.random.key(seed), 15)
    tokens = scatter_about(splits[0], (LEN, SEQS, D), 1.0, 6.0, ((0, 8),))
    attn_gain = jnp.clip(1.0 + 0.1 * jax.random.normal(splits[1], (D,), jnp.float32), 0.5, 1.5)
    qkv_weight = scatter_about(splits[2], (D, 3 * HEADS * HEAD_DIM), D ** -0.5, 0.21875, ((1, 4),))
    bias_table = scatter_about(splits[3], (NB, HEADS), 1.0, 4.0, ((1, 4),), jnp.float32)
    proj_weight = scatter_about(splits[4], (HEADS * HEAD_DIM, D), (max(1, 4 * D // LEN)) ** -0.5, 6.0, ((0, 4),))
    ffn_gain = jnp.clip(1.0 + 0.1 * jax.random.normal(splits[5], (D,), jnp.float32), 0.5, 1.5)
    router_weight = scatter_about(splits[6], (D, EXPERTS), (2 * D) ** -0.5, 0.15625)
    router_bias = scatter_about(splits[7], (EXPERTS,), 0.5, 3.0, (), jnp.float32)
    expert_in = scatter_about(splits[8], (EXPERTS, D, FF), D ** -0.5, 0.21875, ((0, 32),))
    expert_out = scatter_about(splits[9], (EXPERTS, FF, D), (EXPERTS / FF ** 0.5), 6.0, ((0, 32),))
    bucket = set_ends(jax.random.randint(splits[10], (2 * LEN,), 0, NB), jax.random.fold_in(splits[10], 1), 0, NB - 1).astype(jnp.int32)
    expert_choice = draw_expert_choice(jax.random.fold_in(splits[14], 71), 0)
    priority = draw_priority(jax.random.fold_in(splits[14], 71), 0)
    out_grad = scatter_about(splits[13], (LEN, SEQS, D), 1.0, 6.0, ((0, 8), (1, 4)))
    return dict(tokens=tokens, attn_gain=attn_gain, qkv_weight=qkv_weight, bias_table=bias_table, proj_weight=proj_weight, ffn_gain=ffn_gain, router_weight=router_weight, router_bias=router_bias, expert_in=expert_in, expert_out=expert_out, bucket=bucket, expert_choice=expert_choice, priority=priority, out_grad=out_grad)


eps = 1e-06
HIGH = lax.Precision.HIGHEST

@jax.custom_vjp
def low(v):
    return lax.optimization_barrier(v.astype(jnp.bfloat16)).astype(jnp.float32)

@jax.custom_vjp
def low_back(v):
    return v

def low_keep(v):
    return (low(v), None)

def low_pass(kept, grad):
    return (grad,)

def back_keep(v):
    return (v, None)

def back_low(kept, grad):
    return (low(grad),)
low.defvjp(low_keep, low_pass)
low_back.defvjp(back_keep, back_low)

def to_blocks(values):
    shaped = values.reshape((N_SEQ, TSD, N_HEAD, SB) + values.shape[2:])
    return jnp.moveaxis(shaped, 2, 0).reshape((DEVICES, ROWS_MOE) + values.shape[2:])

def from_blocks(values):
    shaped = values.reshape((N_HEAD, N_SEQ, TSD, SB) + values.shape[2:])
    return jnp.moveaxis(shaped, 0, 2).reshape((LEN, SEQS) + values.shape[2:])

def attend_one(item, rel, offsets):
    block, which = item
    query, keys, vals = (block[:, 0], block[:, 1], block[:, 2])
    rel_head = rel[:, which][offsets]
    scores = jnp.einsum('id,jd->ij', query, keys, precision=HIGH) * 0.125 + rel_head
    scores = low_back(scores)
    probs = jax.nn.softmax(scores, axis=-1)
    return jnp.einsum('ij,jd->id', low(probs), vals, precision=HIGH)

def forward(xf, attn_gain, qkv_weight, bias_table, proj_weight, ffn_gain, router_weight, router_bias, expert_in, expert_out, bucket, expert_choice, priority):
    inv1 = lax.rsqrt(lax.optimization_barrier(jnp.mean(xf * xf, axis=-1, keepdims=True)) + eps)
    normed1 = low(xf * inv1 * attn_gain)
    qkv = jnp.einsum('lsd,dc->lsc', normed1, qkv_weight, precision=HIGH)
    qkv = low(low_back(qkv)).reshape(LEN, SEQS, HEADS, 3, HEAD_DIM)
    onehot = (bucket[:, None] == jnp.arange(NB, dtype=jnp.int32)[None, :]).astype(jnp.float32)
    rel = jnp.dot(onehot, bias_table, precision=HIGH)
    where = jnp.arange(LEN, dtype=jnp.int32)
    offsets = (where[None, :] - where[:, None] + LEN).astype(jnp.int32)
    items = jnp.transpose(qkv, (1, 2, 0, 3, 4)).reshape(SEQS * HEADS, LEN, 3, HEAD_DIM)
    which = jnp.tile(jnp.arange(HEADS, dtype=jnp.int32), SEQS)
    per_item = jax.checkpoint(lambda item: attend_one(item, rel, offsets))
    attended = lax.map(per_item, (items, which))
    attended = jnp.transpose(attended.reshape(SEQS, HEADS, LEN, HEAD_DIM), (2, 0, 1, 3))
    attended = low(low_back(attended.reshape(LEN, SEQS, HEADS * HEAD_DIM)))
    branch = low_back(jnp.einsum('lsc,cd->lsd', attended, proj_weight, precision=HIGH))
    mid = xf + branch
    inv2 = lax.rsqrt(lax.optimization_barrier(jnp.mean(mid * mid, axis=-1, keepdims=True)) + eps)
    normed2 = low(mid * inv2 * ffn_gain)
    logits = jnp.einsum('lsd,de->lse', normed2, router_weight, precision=HIGH) + router_bias
    gates = jax.nn.softmax(logits, axis=-1)
    gate = jnp.take_along_axis(gates, expert_choice[..., None], axis=-1)[..., 0]
    sent = to_blocks(low_back(normed2))
    route = to_blocks(expert_choice)
    order = to_blocks(priority)
    same = (route[:, :, None] == route[:, None, :]) & (order[:, None, :] < order[:, :, None])
    rank = lax.optimization_barrier(jnp.sum(same.astype(jnp.int32), axis=2)).astype(jnp.int32)
    keep = (rank < CAP).astype(jnp.float32)
    source = jnp.arange(DEVICES, dtype=jnp.int32)[:, None]
    slot = (source * CAP + jnp.minimum(rank, CAP - 1)).astype(jnp.int32)
    buffer = jnp.zeros((EXPERTS, DEVICES * CAP, D), jnp.float32).at[route, slot].add(sent * keep[..., None])
    pre = low_back(jnp.einsum('esd,edf->esf', buffer, expert_in, precision=HIGH))
    act = low(jax.nn.gelu(pre, approximate=True))
    result = low(low_back(jnp.einsum('esf,efd->esd', act, expert_out, precision=HIGH)))
    expert_rows = from_blocks(result[route, slot] * keep[..., None])
    return mid + gate[..., None] * expert_rows

def reference(tokens, attn_gain, qkv_weight, bias_table, proj_weight, ffn_gain, router_weight, router_bias, expert_in, expert_out, bucket, expert_choice, priority, out_grad):
    floats = tuple((a.astype(jnp.float32) for a in (tokens, attn_gain, qkv_weight, bias_table, proj_weight, ffn_gain, router_weight, router_bias, expert_in, expert_out)))

    def apply_layer(*values):
        return forward(*values, bucket, expert_choice, priority)
    result, pullback = jax.vjp(apply_layer, *floats)
    grads = pullback(out_grad.astype(jnp.float32))
    return (result.astype(jnp.bfloat16), grads[0].astype(jnp.bfloat16), grads[1], grads[2], grads[3], grads[4], grads[5], grads[6], grads[7], grads[8], grads[9])
```

```python
import functools
import math

import jax
import jax.numpy as jnp
from jax import lax
from jax.experimental import pallas as pl
from jax.experimental.pallas import tpu as pltpu
from jax.sharding import PartitionSpec as P

F32 = jnp.float32
BF16 = jnp.bfloat16
LOG2E = math.log2(math.e)
MB = 1024 * 1024
eps = 1e-06
HIGH = lax.Precision.HIGHEST

def nt(a,b): return lax.dot_general(a,b,(((1,),(1,)),((),())),preferred_element_type=F32)
def nn(a,b): return jnp.dot(a,b,preferred_element_type=F32)

def build_strip(win_ref, strip, length, qlen):
    tiles = (length + qlen)//128 - 1
    def one(d, _):
        start = pl.multiple_of(length + qlen - 256 - 128*d, 128)
        u = jnp.broadcast_to(win_ref[0, :, pl.ds(start, 256)], (128, 256))
        strip[pl.ds(pl.multiple_of(d*128,128), 128), :] = pltpu.roll(u, 0, 1, stride=1, stride_axis=0)[:, 128:]
        return 0
    lax.fori_loop(0, tiles, one, 0)

def split3(x):
    hi = x.astype(BF16); r = x - hi.astype(F32)
    mid = r.astype(BF16); lo = (r - mid.astype(F32)).astype(BF16)
    return hi, mid, lo

def rows16(x, n):
    hi, mid, lo = split3(x)
    at = lax.broadcasted_iota(jnp.int32, (16, n), 0)
    z = jnp.zeros((16, n), F32)
    out = jnp.where(at == 0, hi.astype(F32), jnp.where(at == 1, mid.astype(F32), jnp.where(at == 2, lo.astype(F32), z)))
    return out.astype(BF16)

def fwd_kernel(length, qlen, hd, bi, bj, win_ref, q_ref, k_ref, v_ref, out_ref, lse_ref, strip, kaug, qaug, vaug):
    build_strip(win_ref, strip, length, qlen)
    scaled = q_ref[0].astype(F32) * (hd ** -0.5 * LOG2E)
    hi = scaled.astype(BF16)
    qaug[:hd, :] = hi
    qaug[hd:, :] = (scaled - hi.astype(F32)).astype(BF16)
    kk = k_ref[0, 0].T
    kaug[:, :hd] = kk
    kaug[:, hd:] = kk
    vaug[:hd, :] = v_ref[0, 0]
    vaug[hd:, :] = jnp.ones((16, length), BF16)
    def iblock(ib, _):
        i0 = pl.multiple_of(ib*bi, bi)
        q = qaug[:, pl.ds(i0, bi)]
        def jblock(jb, carry):
            m, acc = carry
            j0 = pl.multiple_of(jb*bj, bj)
            s = nn(kaug[pl.ds(j0, bj), :], q)
            bias = [strip[pl.ds(pl.multiple_of(j0 - i0 - 128*c + qlen - 128, 128), bj), :] for c in range(bi//128)]
            s = s + jnp.concatenate(bias, axis=1)
            mn = jnp.maximum(m, jnp.max(s, axis=0, keepdims=True))
            p = jnp.exp2(s - mn).astype(BF16)
            acc = acc * jnp.exp2(m - mn) + nn(vaug[:, pl.ds(j0, bj)], p)
            return mn, acc
        m, acc = lax.fori_loop(0, length//bj, jblock, (jnp.full((1, bi), -1e30, F32), jnp.zeros((hd+16, bi), F32)))
        l = acc[hd:hd+1]
        out_ref[0, :, pl.ds(i0, bi)] = (acc[:hd] / l).astype(BF16)
        lse_ref[0, :, pl.ds(i0, bi)] = m + jnp.log2(l)
        return 0
    lax.fori_loop(0, qlen//bi, iblock, 0)

def attn_fwd(win, qT, kvT, bi=512, bj=512):
    heads, hd, qlen = qT.shape
    length = kvT.shape[3]
    tiles = (length+qlen)//128-1
    return pl.pallas_call(
        functools.partial(fwd_kernel, length, qlen, hd, bi, bj),
        grid=(heads,),
        out_shape=[jax.ShapeDtypeStruct((heads, hd, qlen), BF16), jax.ShapeDtypeStruct((heads, 1, qlen), F32)],
        in_specs=[pl.BlockSpec((1,1,length+qlen), lambda n:(n,0,0)), pl.BlockSpec((1,hd,qlen), lambda n:(n,0,0)),
            pl.BlockSpec((1,1,hd,length), lambda n:(n,1,0,0)), pl.BlockSpec((1,1,hd,length), lambda n:(n,2,0,0))],
        out_specs=[pl.BlockSpec((1,hd,qlen), lambda n:(n,0,0)), pl.BlockSpec((1,1,qlen), lambda n:(n,0,0))],
        scratch_shapes=[pltpu.VMEM((tiles*128,128),F32), pltpu.VMEM((length,2*hd),BF16), pltpu.VMEM((2*hd,qlen),BF16), pltpu.VMEM((hd+16,length),BF16)],
        compiler_params=pltpu.CompilerParams(vmem_limit_bytes=56*MB),
        name="attn_forward",
    )(win, qT, kvT, kvT)

def bwd_kernel(length, qlen, hd, bi, bj, win_ref, q_ref, k_ref, v_ref, o_ref, do_ref, lse_ref,
               dq_ref, dkv_ref, dwin_ref, strip, dstrip, kaug, qaug, vaug, doaug, dk_acc, dv_acc, dwide):
    build_strip(win_ref, strip, length, qlen)
    tiles = (length + qlen)//128 - 1
    scale = hd ** -0.5
    scaled = q_ref[0].astype(F32) * (scale * LOG2E)
    hi = scaled.astype(BF16)
    qaug[:hd, :] = hi
    qaug[hd:2*hd, :] = (scaled - hi.astype(F32)).astype(BF16)
    qaug[2*hd:2*hd+16, :] = rows16(-lse_ref[0], qlen)
    qaug[2*hd+16:, :] = jnp.zeros((2*hd-16, qlen), BF16)
    kk = k_ref[0, 0].T
    kaug[:, :hd] = kk
    kaug[:, hd:2*hd] = kk
    kaug[:, 2*hd:] = jnp.ones((length, 2*hd), BF16)
    vaug[:, :hd] = v_ref[0, 0].T
    vaug[:, hd:] = jnp.ones((length, hd), BF16)
    do = do_ref[0]
    delta = jnp.sum(do.astype(F32) * o_ref[0].astype(F32), axis=0, keepdims=True)
    doaug[:hd, :] = do
    doaug[hd:hd+16, :] = rows16(-delta, qlen)
    doaug[hd+16:, :] = jnp.zeros((hd-16, qlen), BF16)
    dstrip[...] = jnp.zeros_like(dstrip)
    dk_acc[...] = jnp.zeros_like(dk_acc)
    dv_acc[...] = jnp.zeros_like(dv_acc)
    def iblock(ib, _):
        i0 = pl.multiple_of(ib*bi, bi)
        qa = qaug[:, pl.ds(i0, bi)]
        da = doaug[:, pl.ds(i0, bi)]
        q = q_ref[0, :, pl.ds(i0, bi)]
        d = do_ref[0, :, pl.ds(i0, bi)]
        def jblock(jb, dq):
            j0 = pl.multiple_of(jb*bj, bj)
            s = nn(kaug[pl.ds(j0, bj), :], qa)
            at = [pl.ds(pl.multiple_of(j0 - i0 - 128*c + qlen - 128, 128), bj) for c in range(bi//128)]
            p = jnp.exp2(s + jnp.concatenate([strip[a, :] for a in at], axis=1))
            dp = nn(vaug[pl.ds(j0, bj), :], da)
            ds = p * dp
            for c, a in enumerate(at):
                dstrip[a, :] += ds[:, c*128:(c+1)*128]
            dsl = ds.astype(BF16)
            dv_acc[:, pl.ds(j0, bj)] += nt(d, p.astype(BF16))
            dk_acc[:, pl.ds(j0, bj)] += nt(q, dsl)
            return dq + nn(k_ref[0, 0, :, pl.ds(j0, bj)], dsl)
        dq = lax.fori_loop(0, length//bj, jblock, jnp.zeros((hd, bi), F32))
        dq_ref[0, :, pl.ds(i0, bi)] = (dq * scale).astype(BF16)
        return 0
    lax.fori_loop(0, qlen//bi, iblock, 0)
    dkv_ref[0, 0] = (dk_acc[...] * scale).astype(BF16)
    dkv_ref[0, 1] = dv_acc[...].astype(BF16)
    total = length + qlen
    dwide[...] = jnp.zeros_like(dwide)
    def one(d, _):
        start = pl.multiple_of(total - 256 - 128*d, 128)
        t = dstrip[pl.ds(pl.multiple_of(d*128,128), 128), :]
        gathered = jnp.zeros((8, 256), F32)
        for a in range(16):
            wide = jnp.concatenate([jnp.zeros((8,128),F32), t[8*a:8*a+8]], axis=1)
            gathered = gathered + (pltpu.roll(wide, 256 - 8*a, 1) if a else wide)
        dwide[:, pl.ds(start, 256)] += gathered
        return 0
    lax.fori_loop(0, tiles, one, 0)
    x = dwide[...]
    at = lax.broadcasted_iota(jnp.int32, x.shape, 0)
    for bit in (1, 2, 4):
        x = jnp.where((at & bit) != 0, pltpu.roll(x, total - bit, 1), x)
    dwin_ref[0] = jnp.sum(x, axis=0, keepdims=True)

def attn_bwd(win, qT, kvT, oT, doT, lse, bi=512, bj=512):
    heads, hd, qlen = qT.shape
    length = kvT.shape[3]
    tiles = (length+qlen)//128-1
    q_spec = pl.BlockSpec((1,hd,qlen), lambda n:(n,0,0))
    w_spec = pl.BlockSpec((1,1,length+qlen), lambda n:(n,0,0))
    return pl.pallas_call(
        functools.partial(bwd_kernel, length, qlen, hd, bi, bj),
        grid=(heads,),
        out_shape=[jax.ShapeDtypeStruct((heads, hd, qlen), BF16), jax.ShapeDtypeStruct((heads, 2, hd, length), BF16), jax.ShapeDtypeStruct((heads,1,length+qlen),F32)],
        in_specs=[w_spec, q_spec,
            pl.BlockSpec((1,1,hd,length), lambda n:(n,1,0,0)), pl.BlockSpec((1,1,hd,length), lambda n:(n,2,0,0)),
            q_spec, q_spec, pl.BlockSpec((1,1,qlen), lambda n:(n,0,0))],
        out_specs=[q_spec, pl.BlockSpec((1,2,hd,length), lambda n:(n,0,0,0)), w_spec],
        scratch_shapes=[pltpu.VMEM((tiles*128,128),F32), pltpu.VMEM((tiles*128,128),F32), pltpu.VMEM((length,4*hd),BF16), pltpu.VMEM((4*hd,qlen),BF16),
            pltpu.VMEM((length,2*hd),BF16), pltpu.VMEM((2*hd,qlen),BF16), pltpu.VMEM((hd,length),F32), pltpu.VMEM((hd,length),F32), pltpu.VMEM((8,length+qlen),F32)],
        compiler_params=pltpu.CompilerParams(vmem_limit_bytes=56*MB),
        name="attn_backward",
    )(win, qT, kvT, kvT, oT, doT, lse)


MESH = pl.DeviceIdType.MESH


def greet(peers):
    barrier = pltpu.get_barrier_semaphore()
    for peer in peers:
        pl.semaphore_signal(barrier, inc=1, device_id=peer, device_id_type=MESH)
    pl.semaphore_wait(barrier, len(peers))


def remote(source, target, send, recv, peer):
    return pltpu.make_async_remote_copy(
        src_ref=source,
        dst_ref=target,
        send_sem=send,
        recv_sem=recv,
        device_id=peer,
        device_id_type=MESH,
    )


def start_any(source, target, send, recv, peer, is_self):
    @pl.when(is_self)
    def _():
        pltpu.make_async_copy(source, target, recv).start()

    @pl.when(jnp.logical_not(is_self))
    def _():
        remote(source, target, send, recv, peer).start()


def wait_any(source, target, send, recv, peer, is_self):
    remote(source, target, send, recv, peer).wait_recv()

    @pl.when(jnp.logical_not(is_self))
    def _():
        remote(source, target, send, recv, peer).wait_send()


def gather_kernel(n_seq, ways, tsd, piece, rows_in, out, own_sem, a_send, a_recv, p_send, p_recv):
    head, seq = lax.axis_index("head"), lax.axis_index("seq")
    half = lax.rem(seq, ways)
    cross, sibling, beside = (head ^ 2, seq), (head ^ 1, seq), (head, seq ^ 1)
    greet([(head, seq ^ k) for k in range(1, n_seq)] + [cross, sibling])

    def rows_of(k, of_head, of_half):
        at = (seq ^ k) * tsd + (of_head * ways + of_half) * piece
        return out.at[pl.ds(pl.multiple_of(at, piece), piece), :]

    first = []
    for k in range(n_seq):
        to = seq ^ k
        to_half = lax.rem(to, ways)
        source = rows_in.at[lax.div(to, ways), pl.ds(pl.multiple_of(to_half * piece, piece), piece), :]
        at = seq * tsd + (head * ways + to_half) * piece
        target = out.at[pl.ds(pl.multiple_of(at, piece), piece), :]
        if k == 0:
            copy = pltpu.make_async_copy(source, target, own_sem)
        else:
            copy = remote(source, target, a_send.at[k], a_recv.at[k], (head, to))
        copy.start()
        first.append(copy)

    started = []

    def send(kind, k, of_head, of_half, peer, recv_k=None):
        ref = rows_of(k, of_head, of_half)
        copy = remote(ref, ref, p_send.at[kind, k], p_recv.at[kind, k if recv_k is None else recv_k], peer)
        copy.start()
        started.append(copy)

    def arrived(kind, k, of_head, of_half):
        ref = rows_of(k, of_head, of_half)
        remote(ref, ref, p_send.at[kind, k], p_recv.at[kind, k], cross).wait_recv()

    def stage_own(k):
        if k == 0:
            first[0].wait()
        else:
            ref = rows_of(k, head, half)
            remote(ref, ref, a_send.at[k], a_recv.at[k], cross).wait_recv()
        send(0, k, head, half, cross)
        send(1, k, head, half, beside, k ^ 1)
        send(3, k, head, half, sibling)

    def stage_pass(k):
        arrived(0, k, head ^ 2, half)
        arrived(1, k, head, half ^ 1)
        odd = lax.rem(seq ^ k, 2)
        to_head = jnp.where(odd == 1, head ^ 2, head)
        to_seq = jnp.where(odd == 1, seq, seq ^ 1)
        of_head = jnp.where(odd == 1, head, head ^ 2)
        of_half = jnp.where(odd == 1, half ^ 1, half)
        send(2, k, of_head, of_half, (to_head, to_seq), jnp.where(odd == 1, k, k ^ 1))
        send(4, k, head ^ 2, half, sibling)
        send(5, k, head, half ^ 1, sibling)

    def stage_last(k):
        arrived(2, k, head ^ 2, half ^ 1)
        send(6, k, head ^ 2, half ^ 1, sibling)

    for step in range(n_seq + 2):
        if step < n_seq:
            stage_own(step)
        if 1 <= step <= n_seq:
            stage_pass(step - 1)
        if 2 <= step:
            stage_last(step - 2)
    for k in range(n_seq):
        arrived(3, k, head ^ 1, half)
        arrived(4, k, head ^ 3, half)
        arrived(5, k, head ^ 1, half ^ 1)
        arrived(6, k, head ^ 3, half ^ 1)
    for copy in first[1:] + started:
        copy.wait_send()


def gather_rows(rows_in, n_seq, ways, tsd):
    width = rows_in.shape[2]
    piece = rows_in.shape[1] // ways
    return pl.pallas_call(
        functools.partial(gather_kernel, n_seq, ways, tsd, piece),
        out_shape=jax.ShapeDtypeStruct((n_seq * tsd, width), rows_in.dtype),
        in_specs=[pl.BlockSpec(memory_space=pl.ANY)],
        out_specs=pl.BlockSpec(memory_space=pl.ANY),
        scratch_shapes=[
            pltpu.SemaphoreType.DMA,
            pltpu.SemaphoreType.DMA((n_seq,)),
            pltpu.SemaphoreType.DMA((n_seq,)),
            pltpu.SemaphoreType.DMA((7, n_seq)),
            pltpu.SemaphoreType.DMA((7, n_seq)),
        ],
        compiler_params=pltpu.CompilerParams(collective_id=1, has_side_effects=True),
        name="gather_rows",
    )(rows_in)


def to_residual_kernel(own, ways, seqs, n_head, tsd, source, out, send, recv):
    head, seq = lax.axis_index("head"), lax.axis_index("seq")
    batch, half = lax.div(seq, ways), lax.rem(seq, ways)
    to_head = lax.div(batch, own)
    inner = lax.rem(batch, own)
    mine_half = lax.div(seq, seqs)
    mine_at = lax.rem(seq, seqs)
    greet_both(own, ways, seqs, n_head, head, seq)
    calls = []
    for k in range(seqs):
        j = lax.rem(head * own + inner + k, seqs)
        to_seq = half * seqs + j
        is_self = jnp.logical_and(to_head == head, to_seq == seq)
        piece = source.at[:, pl.ds(pl.multiple_of(j * tsd, tsd), tsd)]
        args = (piece, out.at[inner, head], send.at[k], recv.at[k], (to_head, to_seq), is_self)
        start_any(*args)
        calls.append(args)
    for k, args in enumerate(calls):
        number = lax.rem(mine_at - k + seqs, seqs)
        from_head, from_inner = lax.div(number, own), lax.rem(number, own)
        landed = out.at[from_inner, from_head]
        remote(landed, landed, send.at[k], recv.at[k], (to_head, seq)).wait_recv()
        piece, target, sem, arrival, peer, is_self = args

        @pl.when(jnp.logical_not(is_self))
        def _():
            remote(piece, target, sem, arrival, peer).wait_send()


def greet_both(own, ways, seqs, n_head, head, seq):
    batch, half = lax.div(seq, ways), lax.rem(seq, ways)
    inner = lax.rem(batch, own)
    mine_half, mine_at = lax.div(seq, seqs), lax.rem(seq, seqs)
    barrier = pltpu.get_barrier_semaphore()
    for k in range(seqs):
        j = lax.rem(head * own + inner + k, seqs)
        number = lax.rem(mine_at - k + seqs, seqs)
        source_seq = (head * own + lax.rem(number, own)) * ways + mine_half
        for peer in ((lax.div(batch, own), half * seqs + j), (lax.div(number, own), source_seq)):
            pl.semaphore_signal(barrier, inc=1, device_id=peer, device_id_type=MESH)
    pl.semaphore_wait(barrier, 2 * seqs)


def to_residual(source, own, ways, seqs, n_head, tsd):
    rows = source.shape[0]
    return pl.pallas_call(
        functools.partial(to_residual_kernel, own, ways, seqs, n_head, tsd),
        out_shape=jax.ShapeDtypeStruct((own, n_head, rows, tsd), source.dtype),
        in_specs=[pl.BlockSpec(memory_space=pl.ANY)],
        out_specs=pl.BlockSpec(memory_space=pl.ANY),
        scratch_shapes=[pltpu.SemaphoreType.DMA((seqs,)), pltpu.SemaphoreType.DMA((seqs,))],
        compiler_params=pltpu.CompilerParams(collective_id=2, has_side_effects=True),
        name="to_residual",
    )(source)


def to_attention_kernel(own, ways, seqs, n_head, tsd, source, out, send, recv):
    head, seq = lax.axis_index("head"), lax.axis_index("seq")
    batch, half = lax.div(seq, ways), lax.rem(seq, ways)
    inner = lax.rem(batch, own)
    mine_half, mine_at = lax.div(seq, seqs), lax.rem(seq, seqs)
    greet_both(own, ways, seqs, n_head, head, seq)
    lanes = pl.ds(pl.multiple_of(mine_at * tsd, tsd), tsd)
    calls = []
    for k in range(seqs):
        number = lax.rem(mine_at - k + seqs, seqs)
        to_head, to_inner = lax.div(number, own), lax.rem(number, own)
        to_seq = (head * own + to_inner) * ways + mine_half
        is_self = jnp.logical_and(to_head == head, to_seq == seq)
        args = (source.at[to_inner, to_head], out.at[:, lanes], send.at[k], recv.at[k], (to_head, to_seq), is_self)
        start_any(*args)
        calls.append(args)
    for k, args in enumerate(calls):
        j = lax.rem(head * own + inner + k, seqs)
        landed = out.at[:, pl.ds(pl.multiple_of(j * tsd, tsd), tsd)]
        remote(landed, landed, send.at[k], recv.at[k], (head ^ 1, seq)).wait_recv()
        piece, target, sem, arrival, peer, is_self = args

        @pl.when(jnp.logical_not(is_self))
        def _():
            remote(piece, target, sem, arrival, peer).wait_send()


def to_attention(source, own, ways, seqs, n_head, tsd):
    rows = source.shape[2]
    return pl.pallas_call(
        functools.partial(to_attention_kernel, own, ways, seqs, n_head, tsd),
        out_shape=jax.ShapeDtypeStruct((rows, seqs * tsd), source.dtype),
        in_specs=[pl.BlockSpec(memory_space=pl.ANY)],
        out_specs=pl.BlockSpec(memory_space=pl.ANY),
        scratch_shapes=[pltpu.SemaphoreType.DMA((seqs,)), pltpu.SemaphoreType.DMA((seqs,))],
        compiler_params=pltpu.CompilerParams(collective_id=3, has_side_effects=True),
        name="to_attention",
    )(source)


def exchange_kernel(n_head, n_seq, source, out, own_sem, send, recv):
    me = lax.axis_index("head") * n_seq + lax.axis_index("seq")
    devices = n_head * n_seq

    def place(k):
        other = me ^ k
        return lax.div(other, n_seq), lax.rem(other, n_seq)

    greet([place(k) for k in range(1, devices)])
    own = pltpu.make_async_copy(source.at[me], out.at[me], own_sem)
    own.start()
    copies = []
    for k in range(1, devices):
        copy = remote(source.at[me ^ k], out.at[me], send.at[k], recv.at[k], place(k))
        copy.start()
        copies.append(copy)
    own.wait()
    for k, copy in enumerate(copies, 1):
        landed = out.at[me ^ k]
        remote(landed, landed, send.at[k], recv.at[k], place(k)).wait_recv()
        copy.wait_send()


def exchange(source, n_head, n_seq, collective_id, name):
    devices = n_head * n_seq
    return pl.pallas_call(
        functools.partial(exchange_kernel, n_head, n_seq),
        out_shape=jax.ShapeDtypeStruct(source.shape, source.dtype),
        in_specs=[pl.BlockSpec(memory_space=pl.ANY)],
        out_specs=pl.BlockSpec(memory_space=pl.ANY),
        scratch_shapes=[
            pltpu.SemaphoreType.DMA,
            pltpu.SemaphoreType.DMA((devices,)),
            pltpu.SemaphoreType.DMA((devices,)),
        ],
        compiler_params=pltpu.CompilerParams(collective_id=collective_id, has_side_effects=True),
        name=name,
    )(source)


def scatter_kernel(own, ways, groups, parts, out, got1, got2, got3, sum1, sum2, sum3, send, recv, last_send, last_recv):
    head, seq = lax.axis_index("head"), lax.axis_index("seq")
    core, x = lax.rem(head, 2), lax.div(head, 2)
    batch, y = lax.div(seq, ways), lax.rem(seq, ways)
    sibling, cross, beside = (head ^ 1, seq), (head ^ 2, seq), (head, seq ^ 1)
    to_head, inner = lax.div(batch, own), lax.rem(batch, own)
    n_seq = 8 * groups

    def home(v):
        return core * 4 * groups + v * 4 + x * 2 + y

    barrier = pltpu.get_barrier_semaphore()
    peers = [sibling, cross, beside]
    for v in range(groups):
        peers.append((to_head, home(v)))
    from_core, from_v = lax.div(seq, 4 * groups), lax.rem(lax.div(seq, 4), groups)
    from_x, from_y = lax.rem(lax.div(seq, 2), 2), lax.rem(seq, 2)
    for i in range(own):
        peers.append((from_x * 2 + from_core, (head * own + i) * ways + from_y))
    for peer in peers:
        pl.semaphore_signal(barrier, inc=1, device_id=peer, device_id_type=MESH)
    pl.semaphore_wait(barrier, len(peers))

    pending = []

    def go(stage, v, slot, source, target, peer):
        copy = remote(source, target, send.at[stage, v, slot], recv.at[stage, v, slot], peer)
        copy.start()
        pending.append(copy)

    def landed(stage, v, slot, target):
        remote(target, target, send.at[stage, v, slot], recv.at[stage, v, slot], sibling).wait_recv()

    order = [(1, 0, 0), (0, 1, 1), (1, 1, 0), (1, 1, 1), (0, 1, 0), (1, 0, 1), (0, 0, 0), (0, 0, 1)]
    for v in range(groups):
        for slot, (dx, dy, w) in enumerate(order):
            go(0, v, slot, parts.at[1 - core, v, x ^ dx, y ^ dy, w], got1.at[v, slot], sibling)
    for v in range(groups):
        for slot, (dx, dy, w) in enumerate(order):
            landed(0, v, slot, got1.at[v, slot])
            sum1[v, slot] = (
                parts[core, v, x ^ dx, y ^ dy, w].astype(jnp.float32) + got1[v, slot].astype(jnp.float32)
            ).astype(sum1.dtype)
            if w == 0 and dx == 1:
                go(1, v, 1 - dy, sum1.at[v, slot], got2.at[v, 1 - dy], cross)
            if w == 1 and dy == 1:
                go(1, v, 2 + 1 - dx, sum1.at[v, slot], got2.at[v, 2 + 1 - dx], beside)
    kept = {0: (0, 1, 0), 1: (0, 0, 0), 2: (1, 0, 1), 3: (0, 0, 1)}
    for v in range(groups):
        for slot in (0, 2, 1, 3):
            landed(1, v, slot, got2.at[v, slot])
            sum2[v, slot] = (
                sum1[v, order.index(kept[slot])].astype(jnp.float32) + got2[v, slot].astype(jnp.float32)
            ).astype(sum2.dtype)
            if slot == 0:
                go(2, v, 0, sum2.at[v, 0], got3.at[v, 0], beside)
            if slot == 2:
                go(2, v, 1, sum2.at[v, 2], got3.at[v, 1], cross)
    last = []
    for v in range(groups):
        for w in (0, 1):
            landed(2, v, w, got3.at[v, w])
            sum3[v, w] = (
                sum2[v, 1 + 2 * w].astype(jnp.float32) + got3[v, w].astype(jnp.float32)
            ).astype(sum3.dtype)
        is_self = jnp.logical_and(to_head == head, home(v) == seq)
        args = (sum3.at[v], out.at[inner], last_send.at[v], last_recv.at[inner], (to_head, home(v)), is_self)
        start_any(*args)
        last.append(args)
    for i in range(own):
        remote(out.at[i], out.at[i], last_send.at[0], last_recv.at[i], sibling).wait_recv()
    for piece, target, sem, arrival, peer, is_self in last:

        @pl.when(jnp.logical_not(is_self))
        def _():
            remote(piece, target, sem, arrival, peer).wait_send()

    for copy in pending:
        copy.wait_send()


def scatter_sums(parts, own, ways, n_seq, tsd):
    width = parts.shape[-1]
    groups = n_seq // 8
    rows = tsd // 2
    dtype = parts.dtype
    shaped = parts.reshape(2, groups, 2, 2, 2, rows, width)
    out = pl.pallas_call(
        functools.partial(scatter_kernel, own, ways, groups),
        out_shape=jax.ShapeDtypeStruct((own, 2, rows, width), dtype),
        in_specs=[pl.BlockSpec(memory_space=pltpu.VMEM)],
        out_specs=pl.BlockSpec(memory_space=pltpu.VMEM),
        scratch_shapes=[
            pltpu.VMEM((groups, 8, rows, width), dtype),
            pltpu.VMEM((groups, 4, rows, width), dtype),
            pltpu.VMEM((groups, 2, rows, width), dtype),
            pltpu.VMEM((groups, 8, rows, width), dtype),
            pltpu.VMEM((groups, 4, rows, width), dtype),
            pltpu.VMEM((groups, 2, rows, width), dtype),
            pltpu.SemaphoreType.DMA((3, groups, 8)),
            pltpu.SemaphoreType.DMA((3, groups, 8)),
            pltpu.SemaphoreType.DMA((groups,)),
            pltpu.SemaphoreType.DMA((own,)),
        ],
        compiler_params=pltpu.CompilerParams(
            collective_id=6, has_side_effects=True, vmem_limit_bytes=48 * MB
        ),
        name="scatter_sums",
    )(shaped)
    return out.reshape(own, tsd, width)


def reduce_kernel(n_head, n_seq, parts, small, out, small_out, got, own, got_small, own_small, sends, recvs, small_sends, small_recvs):
    head, seq = lax.axis_index("head"), lax.axis_index("seq")
    me = head * n_seq + seq
    devices = n_head * n_seq

    def place(k):
        other = me ^ k
        return lax.div(other, n_seq), lax.rem(other, n_seq)

    greet([place(k) for k in range(1, devices)])
    waits = []
    for k in range(1, devices):
        copy = remote(small.at[me ^ k], got_small.at[k], small_sends.at[0, k], small_recvs.at[0, k], place(k))
        copy.start()
        waits.append(copy)
    for k in range(1, n_seq):
        copy = remote(parts.at[seq ^ k], got.at[k], sends.at[0, k], recvs.at[0, k], (head, seq ^ k))
        copy.start()
        waits.append(copy)
    total = small[me]
    for k in range(1, devices):
        remote(got_small.at[k], got_small.at[k], small_sends.at[0, k], small_recvs.at[0, k], place(k)).wait_recv()
        total = total + got_small[k]
    own_small[...] = total
    small_out[me] = total
    for k in range(1, devices):
        copy = remote(own_small, small_out.at[me], small_sends.at[1, k], small_recvs.at[1, k], place(k))
        copy.start()
        waits.append(copy)
    total = parts[seq].astype(jnp.float32)
    for k in range(1, n_seq):
        remote(got.at[k], got.at[k], sends.at[0, k], recvs.at[0, k], (head, seq ^ k)).wait_recv()
        total = total + got[k].astype(jnp.float32)
    own[...] = total.astype(own.dtype)
    out[seq] = total.astype(own.dtype)
    for k in range(1, n_seq):
        copy = remote(own, out.at[seq], sends.at[1, k], recvs.at[1, k], (head, seq ^ k))
        copy.start()
        waits.append(copy)
    for k in range(1, devices):
        landed = small_out.at[me ^ k]
        remote(landed, landed, small_sends.at[1, k], small_recvs.at[1, k], place(k)).wait_recv()
    for k in range(1, n_seq):
        landed = out.at[seq ^ k]
        remote(landed, landed, sends.at[1, k], recvs.at[1, k], (head, seq ^ k)).wait_recv()
    for copy in waits:
        copy.wait_send()


def reduce_weights(parts, small, n_head, n_seq):
    devices = n_head * n_seq
    rows, width = parts.shape[1:]
    whole = pl.BlockSpec(memory_space=pltpu.VMEM)
    return pl.pallas_call(
        functools.partial(reduce_kernel, n_head, n_seq),
        out_shape=[
            jax.ShapeDtypeStruct(parts.shape, parts.dtype),
            jax.ShapeDtypeStruct(small.shape, small.dtype),
        ],
        in_specs=[whole, whole],
        out_specs=[whole, whole],
        scratch_shapes=[
            pltpu.VMEM((n_seq, rows, width), parts.dtype),
            pltpu.VMEM((rows, width), parts.dtype),
            pltpu.VMEM((devices, 8, 128), small.dtype),
            pltpu.VMEM((8, 128), small.dtype),
            pltpu.SemaphoreType.DMA((2, n_seq)),
            pltpu.SemaphoreType.DMA((2, n_seq)),
            pltpu.SemaphoreType.DMA((2, devices)),
            pltpu.SemaphoreType.DMA((2, devices)),
        ],
        compiler_params=pltpu.CompilerParams(
            collective_id=7, has_side_effects=True, vmem_limit_bytes=32 * MB
        ),
        name="reduce_weights",
    )(parts, small)


def rms_inverse(values):
    return lax.rsqrt(jnp.mean(values * values, axis=-1, keepdims=True) + eps)


def dot(a, b, dims, precision=None):
    return lax.dot_general(a, b, (dims, ((), ())), preferred_element_type=F32, precision=precision)


def local(
    n_head,
    n_seq,
    tokens,
    attn_gain,
    qkv_weight,
    bias_table,
    proj_weight,
    ffn_gain,
    router_weight,
    router_bias,
    expert_in,
    expert_out,
    bucket,
    expert_choice,
    priority,
    out_grad,
):
    tsd, seqs, width = tokens.shape
    buckets, heads_here = bias_table.shape
    head_dim = qkv_weight.shape[1] // (3 * heads_here)
    hidden = heads_here * head_dim
    length = bucket.shape[0] // 2
    own = out_grad.shape[1]
    ways = n_seq // seqs
    qlen = length // ways
    experts = router_weight.shape[1]
    devices = n_head * n_seq
    assert ways == 2 and n_head == 4 and own * n_head == seqs and experts == devices
    seq_index = lax.axis_index("seq")
    head_index = lax.axis_index("head")
    half = seq_index % ways

    share = tsd // n_head
    x_share = lax.dynamic_slice_in_dim(tokens, head_index * share, share, 0).astype(F32)
    n_share = (x_share * rms_inverse(x_share) * attn_gain).astype(BF16)
    normed1 = gather_rows(jnp.moveaxis(n_share, 1, 0), n_seq, ways, tsd)

    proj_full = lax.all_gather(proj_weight, "head", axis=0, tiled=True)

    reversed_bucket = jnp.concatenate([bucket[:1], bucket[:0:-1]])
    near = lax.dynamic_slice_in_dim(reversed_bucket, half * qlen, length + qlen, 0)
    onehot = (near[None, :] == jnp.arange(buckets, dtype=jnp.int32)[:, None]).astype(F32)
    window = dot(bias_table * LOG2E, onehot, ((0,), (0,)), HIGH)[:, None, :]

    qkv_t = dot(qkv_weight, normed1, ((0,), (1,))).astype(BF16)
    qkv_t = qkv_t.reshape(heads_here, 3, head_dim, length)
    query_t = lax.dynamic_slice_in_dim(qkv_t[:, 0], half * qlen, qlen, 2)
    attended_t, lse = attn_fwd(window, query_t, qkv_t, 1024, 1024)

    spread = to_residual(attended_t.reshape(hidden, qlen), own, ways, seqs, n_head, tsd)
    att_all = spread.reshape(own, n_head * hidden, tsd)
    branch = jnp.einsum("bcp,cd->bpd", att_all, proj_full, preferred_element_type=F32)
    rows = own * tsd
    x_own = lax.dynamic_slice_in_dim(tokens, head_index * own, own, 1).astype(F32)
    x_own = jnp.moveaxis(x_own, 1, 0).reshape(rows, width)
    inv1 = rms_inverse(x_own)
    mid = x_own + branch.reshape(rows, width)
    inv2 = rms_inverse(mid)
    normed2 = (mid * inv2 * ffn_gain).astype(BF16)
    logits = dot(normed2, router_weight, ((1,), (0,))) + router_bias
    gates = jax.nn.softmax(logits, axis=1)
    route = expert_choice.T.reshape(rows)
    order = priority.T.reshape(rows)
    same = (route[:, None] == route[None, :]) & (order[None, :] < order[:, None])
    rank = jnp.sum(same.astype(jnp.int32), axis=1)
    capacity = max(2, (5 * rows + 4 * experts - 1) // (4 * experts))
    slots = (capacity + 7) // 8 * 8
    keep = rank < capacity
    chosen = (route[:, None] == jnp.arange(experts, dtype=jnp.int32)[None, :]).astype(F32)
    gate = jnp.sum(gates * chosen, axis=1)
    upstream = jnp.moveaxis(out_grad, 1, 0).astype(F32).reshape(rows, width)
    grad_rows = (gate[:, None] * upstream).astype(BF16)
    slot = jnp.where(keep, route * (2 * slots) + rank, -1)
    slot = jnp.concatenate([slot, jnp.where(keep, slot + slots, -1)])
    placing = (slot[None, :] == jnp.arange(experts * 2 * slots, dtype=jnp.int32)[:, None]).astype(BF16)
    sending = dot(placing, jnp.concatenate([normed2, grad_rows], axis=0), ((1,), (0,))).astype(BF16)
    arriving = exchange(sending.reshape(devices, 2 * slots, width), n_head, n_seq, 4, "to_experts")

    arriving = arriving.reshape(devices, 2, slots, width)
    came = arriving[:, 0].reshape(devices * slots, width)
    came_grad = arriving[:, 1].reshape(devices * slots, width)
    pre = dot(came, expert_in[0], ((1,), (0,)))
    act_value, act_pull = jax.vjp(lambda v: jax.nn.gelu(v, approximate=True), pre)
    act = act_value.astype(BF16)
    result = dot(act, expert_out[0], ((1,), (0,))).astype(BF16)
    grad_act = dot(came_grad, expert_out[0], ((1,), (1,)))
    grad_pre = act_pull(grad_act)[0].astype(BF16)
    grad_slots = dot(grad_pre, expert_in[0], ((1,), (1,))).astype(BF16)
    grad_expert_out = dot(act, came_grad, ((0,), (0,)))[None]
    grad_expert_in = dot(came, grad_pre, ((0,), (0,)))[None]
    returning = jnp.stack(
        [result.reshape(devices, slots, width), grad_slots.reshape(devices, slots, width)], axis=1
    )
    back = exchange(returning.reshape(devices, 2 * slots, width), n_head, n_seq, 5, "from_experts")
    placed = dot(placing, back.reshape(devices * 2 * slots, width), ((0,), (0,)))
    expert_rows, grad_disp = placed[:rows], placed[rows:]

    output = mid + gate[:, None] * expert_rows
    output = jnp.moveaxis(output.astype(BF16).reshape(own, tsd, width), 0, 1)
    grad_gate = jnp.sum(upstream * expert_rows, axis=1)
    grad_logits = gates * (chosen - gate[:, None]) * grad_gate[:, None]
    grad_router_bias = jnp.sum(grad_logits, axis=0)
    grad_router_t = dot(grad_logits, normed2.astype(F32), ((0,), (0,)), HIGH)
    grad_normed2 = grad_disp + dot(grad_logits, router_weight.astype(F32), ((1,), (1,)), HIGH)
    scaled2 = grad_normed2 * ffn_gain
    unit2 = mid * inv2
    grad_ffn_gain = jnp.sum(grad_normed2 * unit2, axis=0)
    grad_mid = upstream + inv2 * (scaled2 - unit2 * jnp.mean(scaled2 * unit2, axis=-1, keepdims=True))
    grad_branch = grad_mid.astype(BF16).reshape(own, tsd, width)

    grad_att = jnp.einsum("cd,bpd->bcp", proj_full, grad_branch, preferred_element_type=F32)
    grad_att = grad_att.astype(BF16).reshape(own, n_head, hidden, tsd)
    grad_attended_t = to_attention(grad_att, own, ways, seqs, n_head, tsd)
    grad_proj = jnp.einsum("bcp,bpd->cd", att_all, grad_branch, preferred_element_type=F32)
    grad_proj = lax.psum_scatter(grad_proj.astype(BF16), "head", scatter_dimension=0, tiled=True)

    grad_q, grad_kv, grad_window = attn_bwd(
        window, query_t, qkv_t, attended_t, grad_attended_t.reshape(heads_here, head_dim, qlen), lse, 512, 1024
    )
    grad_table = dot(onehot, grad_window[:, 0], ((1,), (1,)), HIGH)
    wide_q = lax.dynamic_update_slice_in_dim(
        jnp.zeros((heads_here, head_dim, length), BF16), grad_q, half * qlen, 2
    )
    grad_qkv_t = jnp.concatenate([wide_q[:, None], grad_kv], axis=1).reshape(3 * hidden, length)
    grad_normed1 = dot(grad_qkv_t, qkv_weight, ((0,), (1,))).astype(BF16)
    grad_weight_t = dot(grad_qkv_t, normed1, ((1,), (0,)))
    grad_gain_part = jnp.sum(grad_weight_t * qkv_weight.T.astype(F32), axis=0)

    parts = jnp.concatenate([grad_weight_t.astype(BF16), grad_proj], axis=0)
    piece = -(-parts.shape[0] // (16 * n_seq)) * 16
    parts = jnp.pad(parts, ((0, piece * n_seq - parts.shape[0]), (0, 0)))
    table_whole = lax.dynamic_update_slice_in_dim(
        jnp.zeros((buckets, n_head * heads_here), F32), grad_table, head_index * heads_here, 1
    )
    extras = jnp.concatenate([grad_ffn_gain, grad_gain_part, grad_router_bias, table_whole.reshape(-1)])
    lanes = 128
    chunks = width // lanes
    extras = jnp.pad(extras, (0, devices * (8 - chunks) * lanes - extras.shape[0]))
    small = jnp.concatenate(
        [grad_router_t.reshape(experts, chunks, lanes), extras.reshape(devices, 8 - chunks, lanes)], axis=1
    )
    reduced, small = reduce_weights(parts.reshape(n_seq, piece, width), small, n_head, n_seq)
    reduced = reduced.reshape(n_seq * piece, width)
    grad_qkv_weight = reduced[: 3 * hidden].T.astype(F32)
    grad_proj_weight = reduced[3 * hidden : 3 * hidden + hidden].astype(F32)
    grad_router_weight = small[:, :chunks].reshape(experts, width).T
    extras = small[:, chunks:].reshape(-1)
    grad_ffn_gain = extras[:width]
    grad_attn_gain = extras[width : 2 * width] / attn_gain
    grad_router_bias = extras[2 * width : 2 * width + experts]
    table_whole = extras[2 * width + experts :][: buckets * n_head * heads_here]
    grad_bias_table = lax.dynamic_slice_in_dim(
        table_whole.reshape(buckets, n_head * heads_here), head_index * heads_here, heads_here, 1
    )

    grad_normed1_own = scatter_sums(grad_normed1, own, ways, n_seq, tsd).reshape(rows, width).astype(F32)
    unit1 = x_own * inv1
    scaled1 = grad_normed1_own * attn_gain
    grad_x = inv1 * (scaled1 - unit1 * jnp.mean(scaled1 * unit1, axis=-1, keepdims=True))
    grad_tokens = (grad_mid + grad_x).astype(BF16)
    grad_tokens = jnp.moveaxis(grad_tokens.reshape(own, tsd, width), 0, 1)
    return (
        output,
        grad_tokens,
        grad_attn_gain,
        grad_qkv_weight,
        grad_bias_table,
        grad_proj_weight,
        grad_ffn_gain,
        grad_router_weight,
        grad_router_bias,
        grad_expert_in,
        grad_expert_out,
    )


def solution(mesh):
    placed = (
        P("seq", None, None),
        P(),
        P(None, "head"),
        P(None, "head"),
        P("head", None),
        P(),
        P(),
        P(),
        P(("head", "seq"), None, None),
        P(("head", "seq"), None, None),
        P(),
        P("seq", "head"),
        P("seq", "head"),
        P("seq", "head", None),
    )
    return jax.shard_map(
        functools.partial(local, mesh.shape["head"], mesh.shape["seq"]),
        mesh=mesh,
        in_specs=placed,
        out_specs=(
            P("seq", "head", None),
            P("seq", "head", None),
            P(),
            P(None, "head"),
            P(None, "head"),
            P("head", None),
            P(),
            P(),
            P(),
            P(("head", "seq"), None, None),
            P(("head", "seq"), None, None),
        ),
        check_vma=False,
    )
```

```python
import functools
import math

import jax
import jax.numpy as jnp
from jax import lax
from jax.experimental import pallas as pl
from jax.experimental.pallas import tpu as pltpu
from jax.sharding import PartitionSpec as P

F32 = jnp.float32
BF16 = jnp.bfloat16
LOG2E = math.log2(math.e)
MB = 1024 * 1024
eps = 1e-06
HIGH = lax.Precision.HIGHEST

def nt(a, b):
    return lax.dot_general(a, b, (((1,), (1,)), ((), ())), preferred_element_type=F32)


def nn(a, b):
    return jnp.dot(a, b, preferred_element_type=F32)


def biases(bucket, table):
    count = table.shape[1]
    row, column = (lax.broadcasted_iota(jnp.int32, (count, count), n) for n in (0, 1))
    table = jnp.sum(jnp.where(row == column, table, 0.0), axis=1, keepdims=True)
    same = bucket == lax.broadcasted_iota(jnp.int32, (count, bucket.shape[1]), 0)
    return jnp.sum(jnp.where(same, table * LOG2E, 0.0), axis=0, keepdims=True)


def turned(window):
    total = window.shape[1]
    base = pltpu.roll(jnp.broadcast_to(window, (8, total)), 0, 1, stride=1, stride_axis=0)
    return [pltpu.roll(base, 8 * a, 1) if a else base for a in range(16)]


def build_strip(window, strip):
    total = window.shape[1]
    for a, rows in enumerate(turned(window)):
        for d in range(total // 128 - 1):
            at = total - 128 - 128 * d
            strip[d * 128 + 8 * a : d * 128 + 8 * a + 8, :] = rows[:, at : at + 128]


def build_transposed(window, strip, wide):
    for a, rows in enumerate(turned(window)):
        wide[8 * a : 8 * a + 8, :] = rows
    for d in range(window.shape[1] // 128 - 1):
        strip[d * 128 : d * 128 + 128, :] = wide[:, 128 * d + 128 : 128 * d + 256].T


def fold_strip(strip, total):
    tiles = total // 128 - 1
    folded = jnp.zeros((8, total), F32)
    for a in range(16):
        pieces = [jnp.zeros((8, 128), F32)]
        for d in range(tiles - 1, -1, -1):
            pieces.append(strip[d * 128 + 8 * a : d * 128 + 8 * a + 8, :])
        wide = jnp.concatenate(pieces, axis=1)
        folded = folded + (pltpu.roll(wide, total - 8 * a, 1) if a else wide)
    at = lax.broadcasted_iota(jnp.int32, folded.shape, 0)
    for bit in (1, 2, 4):
        folded = jnp.where((at & bit) != 0, pltpu.roll(folded, total - bit, 1), folded)
    return jnp.sum(folded, axis=0, keepdims=True)


def three_rows(x):
    high = x.astype(BF16).astype(F32)
    mid = (x - high).astype(BF16).astype(F32)
    at = lax.broadcasted_iota(jnp.int32, (16, x.shape[1]), 0)
    rows = jnp.where(at == 0, high, jnp.where(at == 1, mid, jnp.where(at == 2, x - high - mid, 0.0)))
    return rows.astype(BF16)


def position(i, tsd, ways, half):
    return (i // tsd * ways + half) * tsd + i % tsd


def own_queries(q_ref, tsd, ways, half):
    blocks = q_ref.shape[3] // (tsd * ways)
    at = [pl.multiple_of((n * ways + half) * tsd, tsd) for n in range(blocks)]
    return jnp.concatenate([q_ref[0, 0, :, pl.ds(a, tsd)] for a in at], axis=1)


def forward_kernel(
    length, qlen, hd, tsd, bi, bj, half_ref, strip_ref, q_ref, k_ref, v_ref, out_ref, lse_ref, kaug, qaug, vaug
):
    ways = length // qlen
    half = half_ref[0]
    strip = strip_ref.at[0]
    scaled = own_queries(q_ref, tsd, ways, half).astype(F32) * (hd**-0.5 * LOG2E)
    high = scaled.astype(BF16)
    qaug[:hd, :] = high
    qaug[hd:, :] = (scaled - high.astype(F32)).astype(BF16)
    keys = k_ref[0, 0].T
    kaug[:, :hd] = keys
    kaug[:, hd:] = keys
    vaug[:hd, :] = v_ref[0, 0]
    vaug[hd:, :] = jnp.ones((16, length), BF16)

    def scores(i0, j0):
        raw = nn(kaug[pl.ds(j0, bj), :], qaug[:, pl.ds(i0, bi)])
        at = [j0 - position(i0 + 128 * c, tsd, ways, half) + length - 128 for c in range(bi // 128)]
        bias = [strip[pl.ds(pl.multiple_of(a, 128), bj), :] for a in at]
        return raw + jnp.concatenate(bias, axis=1)

    def store(i0, top, acc):
        total = acc[hd : hd + 1]
        out_ref[0, :, pl.ds(i0, bi)] = (acc[:hd] / total).astype(BF16)
        lse_ref[0, :, pl.ds(i0, bi)] = top + jnp.log2(total)
        return total

    def quick(ib, bounds):
        i0 = pl.multiple_of(ib * bi, bi)
        acc = jnp.zeros((hd + 16, bi), F32)
        for jb in range(length // bj):
            p = jnp.exp2(scores(i0, jb * bj)).astype(BF16)
            acc = acc + nn(vaug[:, jb * bj : (jb + 1) * bj], p)
        total = store(i0, 0.0, acc)
        return jnp.minimum(bounds[0], total), jnp.maximum(bounds[1], total)

    one = jnp.ones((1, bi), F32)
    low, high = lax.fori_loop(0, qlen // bi, quick, (one, one))
    fine = jnp.logical_and(jnp.min(low) > 2.0**-90, jnp.max(high) < 2.0**90)

    @pl.when(jnp.logical_not(fine))
    def _():
        def careful(ib, _):
            i0 = pl.multiple_of(ib * bi, bi)

            def step(jb, carry):
                top, acc = carry
                j0 = pl.multiple_of(jb * bj, bj)
                s = scores(i0, j0)
                new = jnp.maximum(top, jnp.max(s, axis=0, keepdims=True))
                p = jnp.exp2(s - new).astype(BF16)
                return new, acc * jnp.exp2(top - new) + nn(vaug[:, pl.ds(j0, bj)], p)

            start = (jnp.full((1, bi), -3e38, F32), jnp.zeros((hd + 16, bi), F32))
            store(i0, *lax.fori_loop(0, length // bj, step, start))
            return 0

        lax.fori_loop(0, qlen // bi, careful, 0)


def attend_forward(half, strips, qkv_t, qlen, tsd, bi=2048, bj=512):
    heads, _, hd, length = qkv_t.shape
    return pl.pallas_call(
        functools.partial(forward_kernel, length, qlen, hd, tsd, bi, bj),
        grid=(heads,),
        out_shape=[
            jax.ShapeDtypeStruct((heads, hd, qlen), BF16),
            jax.ShapeDtypeStruct((heads, 1, qlen), F32),
        ],
        in_specs=[
            pl.BlockSpec(memory_space=pltpu.SMEM),
            pl.BlockSpec((1,) + strips.shape[1:], lambda n: (n, 0, 0)),
            pl.BlockSpec((1, 1, hd, length), lambda n: (n, 0, 0, 0)),
            pl.BlockSpec((1, 1, hd, length), lambda n: (n, 1, 0, 0)),
            pl.BlockSpec((1, 1, hd, length), lambda n: (n, 2, 0, 0)),
        ],
        out_specs=[
            pl.BlockSpec((1, hd, qlen), lambda n: (n, 0, 0)),
            pl.BlockSpec((1, 1, qlen), lambda n: (n, 0, 0)),
        ],
        scratch_shapes=[
            pltpu.VMEM((length, 2 * hd), BF16),
            pltpu.VMEM((2 * hd, qlen), BF16),
            pltpu.VMEM((hd + 16, length), BF16),
        ],
        compiler_params=pltpu.CompilerParams(vmem_limit_bytes=56 * MB),
        cost_estimate=pl.CostEstimate(
            flops=4 * heads * hd * qlen * length,
            bytes_accessed=10 * heads * hd * length,
            transcendentals=heads * qlen * length,
        ),
        name="attend_forward",
    )(half, strips, qkv_t, qkv_t, qkv_t)


def sum_over_seq(head, seq, parts, got_y, sum_y, got_z, own_z, out, y_send, y_recv, z_send, z_recv):
    line, pair = lax.div(seq, 2), lax.rem(seq, 2)
    lines = parts.shape[0]
    beside = (head, seq ^ 1)
    far = [(k, (head, seq ^ (2 * k))) for k in range(1, lines)]
    mine = out.at[line, pair]

    def over_pair():
        return remote(parts.at[:, 1 - pair], got_y, y_send.at[0], y_recv.at[0], beside)

    def over_line(k, peer):
        return remote(sum_y.at[line ^ k], got_z.at[k], z_send.at[0, k], z_recv.at[0, k], peer)

    def back_line(k, peer):
        return remote(own_z, mine, z_send.at[1, k], z_recv.at[1, k], peer)

    def back_pair():
        return remote(own_z, mine, y_send.at[1], y_recv.at[1], beside)

    def pass_on(k):
        passed = out.at[line ^ k, pair]
        return remote(passed, passed, y_send.at[1 + k], y_recv.at[1 + k], beside)

    def first():
        over_pair().start()

    def second():
        over_pair().wait()
        for p in range(lines):
            sum_y[p] = (parts[p, pair].astype(F32) + got_y[p].astype(F32)).astype(BF16)
        for k, peer in far:
            over_line(k, peer).start()

    def third():
        total = sum_y[line].astype(F32)
        for k, peer in far:
            over_line(k, peer).wait()
            total = total + got_z[k].astype(F32)
        own_z[...] = total.astype(BF16)
        out[line, pair] = total.astype(BF16)
        for k, peer in far:
            back_line(k, peer).start()
        back_pair().start()

    def fourth():
        for k, peer in far:
            landed = out.at[line ^ k, pair]
            remote(landed, landed, z_send.at[1, k], z_recv.at[1, k], peer).wait_recv()
            pass_on(k).start()

    def fifth():
        for k, peer in far:
            back_line(k, peer).wait_send()
            pass_on(k).wait_send()
        back_pair().wait_send()
        for k in range(lines):
            landed = out.at[line ^ k, 1 - pair]
            remote(landed, landed, y_send.at[1 + k], y_recv.at[1 + k], beside).wait_recv()

    return first, second, third, fourth, fifth


def backward_kernel(
    length, qlen, hd, tsd, bi, bj, own, seqs, n_head, buckets,
    bucket_ref, strip_ref, q_ref, k_ref, v_ref, o_ref, lse_ref, w_ref, att, grad_branch, proj, normed,
    grad_ref, grad_table_ref, gain_ref, reduced, last,
    source, att_v, branch_v, weight_v, dstrip, kaug, qaug, vaug, daug, q_v, dk_acc, dv_acc, do_ref,
    rows_v, proj_v, got_p, pass_p, got_q, proj_sum, parts, got_y, sum_y, got_z, own_z, sums,
    send, recv, load_sem, p_send, p_recv, y_send, y_recv, z_send, z_recv,
):
    total = 2 * length
    ways = length // qlen
    head, seq = lax.axis_index("head"), lax.axis_index("seq")
    half = lax.rem(seq, ways)
    item = pl.program_id(0)
    heads = pl.num_programs(0)
    inner = line_to_batch(lax.div(seq, ways), seqs) % own
    mine = pl.multiple_of(lax.div(seq, ways) * tsd, tsd)

    def peer(k):
        number = lax.rem(lax.div(seq, ways) - k + seqs, seqs)
        to_head, to_inner = lax.div(number, own), lax.rem(number, own)
        to_seq = batch_to_line(head * own + to_inner, seqs) * ways + half
        return to_head, to_inner, to_seq, jnp.logical_and(to_head == head, to_seq == seq)

    def piece(k, n):
        to_head, to_inner, to_seq, is_self = peer(k)
        target = do_ref.at[n, :, pl.ds(mine, tsd)]
        return source.at[to_inner, to_head, n], target, send.at[k, n], recv.at[k, n], (to_head, to_seq), is_self

    sibling, cross = (head ^ 1, seq), (head ^ 2, seq)
    lines = parts.shape[1]
    others = [(head, seq ^ (2 * k)) for k in range(1, lines)] + [(head, seq ^ 1), sibling, cross]
    loads = [
        pltpu.make_async_copy(normed, rows_v, load_sem.at[0]),
        pltpu.make_async_copy(proj, weight_v, load_sem.at[1]),
        pltpu.make_async_copy(grad_branch, branch_v, load_sem.at[2]),
        pltpu.make_async_copy(att, att_v, load_sem.at[3]),
    ]
    hidden = proj_v.shape[1]

    @pl.when(item == 0)
    def _():
        for load in (loads[1], loads[2], loads[3], loads[0]):
            load.start()
        greet_both(own, ways, seqs, n_head, head, seq, others, wait=False)
        loads[1].wait()
        loads[2].wait()
        for b in range(own):
            grads = nt(weight_v[...], branch_v[b]).astype(BF16)
            for h in range(n_head):
                for n in range(source.shape[2]):
                    at = h * hidden + n * hd
                    source[b, h, n] = grads[at : at + hd]
        pl.semaphore_wait(pltpu.get_barrier_semaphore(), 2 * seqs + len(others))
        for k in range(seqs):
            start_any(*piece(k, 0))
        loads[3].wait()
        total = functools.reduce(jnp.add, [nn(att_v[b], branch_v[b]) for b in range(own)]).astype(BF16)
        for h in range(n_head):
            proj_v[h] = total[h * hidden : (h + 1) * hidden]
        for n, of in enumerate((1, 3)):
            remote(proj_v.at[head ^ of], got_p.at[n], p_send.at[n], p_recv.at[n], sibling).start()

    def proj_over_x():
        for n in range(2):
            remote(got_p.at[n], got_p.at[n], p_send.at[n], p_recv.at[n], sibling).wait()
        pass_p[...] = (proj_v[head ^ 2].astype(F32) + got_p[1].astype(F32)).astype(BF16)
        remote(pass_p, got_q, p_send.at[2], p_recv.at[2], cross).start()

    def proj_total():
        remote(pass_p, got_q, p_send.at[2], p_recv.at[2], cross).wait()
        total = proj_v[head].astype(F32) + got_p[0].astype(F32) + got_q[...].astype(F32)
        proj_sum[...] = total.astype(BF16)
        loads[0].wait()

    def stages(m):
        return sum_over_seq(
            head, seq, parts.at[m], got_y.at[m], sum_y.at[m], got_z.at[m], own_z.at[m], sums.at[m],
            y_send.at[m], y_recv.at[m], z_send.at[m], z_recv.at[m],
        )

    strip = strip_ref.at[0]
    scale = hd**-0.5
    q_v[...] = own_queries(q_ref, tsd, ways, half)
    scaled = q_v[...].astype(F32) * (scale * LOG2E)
    high = scaled.astype(BF16)
    rest = (scaled - high.astype(F32)).astype(BF16)
    blank = jnp.zeros((2 * hd - 16, qlen), BF16)
    qaug[...] = jnp.concatenate([high, rest, three_rows(-lse_ref[0]), blank], axis=0).T
    keys = k_ref[0, 0]
    kaug[:hd, :] = keys
    kaug[hd : 2 * hd, :] = keys
    kaug[2 * hd :, :] = jnp.ones((2 * hd, length), BF16)
    vaug[:hd, :] = v_ref[0, 0]
    vaug[hd:, :] = jnp.ones((hd, length), BF16)
    for k in range(seqs):
        j = lax.rem(head * own + inner + k, seqs)
        landed = do_ref.at[item, :, pl.ds(pl.multiple_of(j * tsd, tsd), tsd)]
        remote(landed, landed, send.at[k, item], recv.at[k, item], (head ^ 1, seq)).wait_recv()

    @pl.when(item < heads - 1)
    def _():
        for k in range(seqs):
            start_any(*piece(k, item + 1))

    do = do_ref[item]
    delta = jnp.sum(do.astype(F32) * o_ref[0].astype(F32), axis=0, keepdims=True)
    daug[...] = jnp.concatenate([do, three_rows(-delta), blank[: hd - 16]], axis=0).T
    dstrip[...] = jnp.zeros_like(dstrip)
    dk_acc[...] = jnp.zeros_like(dk_acc)
    dv_acc[...] = jnp.zeros_like(dv_acc)
    grad_ref[0, :hd, :] = jnp.zeros((hd, length), BF16)
    across = bj // 128
    run = min(bi, tsd)
    down = run // 128

    def rows(i, j0, count):
        return pl.ds(pl.multiple_of(i - j0 + length - 128, 128), count)

    before = stages(jnp.maximum(item - 1, 0))
    assert qlen // bi >= 4

    def step(ib, _):
        i0 = pl.multiple_of(ib * bi, bi)
        here = pl.ds(i0, bi)
        for n in (1, 2, 3):

            @pl.when(jnp.logical_and(item > 0, ib == n))
            def _():
                before[n]()

        @pl.when(jnp.logical_and(item == 0, ib == 1))
        def _():
            proj_over_x()

        places = [position(i0 + m * run, tsd, ways, half) for m in range(bi // run)]
        dq = jnp.zeros((hd, bi), F32)
        for jb in range(length // bj):
            j0 = jb * bj
            there = slice(j0, j0 + bj)
            s = nn(qaug[here, :], kaug[:, there])
            bias = [
                jnp.concatenate([strip[rows(i, j0 + 128 * c, run), :] for c in range(across)], axis=1)
                for i in places
            ]
            p = jnp.exp2(s + jnp.concatenate(bias, axis=0))
            ds = p * nn(daug[here, :], vaug[:, there])
            for m, i in enumerate(places):
                for g in range(1 - across, down):
                    parts = [
                        ds[m * run + a * 128 : m * run + (a + 1) * 128, (a - g) * 128 : (a - g + 1) * 128]
                        for a in range(down)
                        if 0 <= a - g < across
                    ]
                    dstrip[rows(i + 128 * g, j0, 128), :] += functools.reduce(jnp.add, parts)
            dsl = ds.astype(BF16)
            dv_acc[:, there] += nn(do_ref[item, :, here], p.astype(BF16))
            dk_acc[:, there] += nn(q_v[:, here], dsl)
            dq = dq + nt(k_ref[0, 0, :, there], dsl)
        dq = (dq * scale).astype(BF16)
        for m, i in enumerate(places):
            grad_ref[0, :hd, pl.ds(pl.multiple_of(i, run), run)] = dq[:, m * run : (m + 1) * run]
        return 0

    lax.fori_loop(0, qlen // bi, step, 0)
    grad_ref[0, hd : 2 * hd, :] = (dk_acc[...] * scale).astype(BF16)
    grad_ref[0, 2 * hd :, :] = dv_acc[...].astype(BF16)
    same = bucket_ref[...] == lax.broadcasted_iota(jnp.int32, (buckets, total), 0)
    table = jnp.sum(jnp.where(same, fold_strip(dstrip, total), 0.0), axis=1, keepdims=True)
    row, column = (lax.broadcasted_iota(jnp.int32, (buckets, 128), n) for n in (0, 1))
    table = jnp.sum(jnp.where(row == column, table, 0.0), axis=0, keepdims=True)
    grad_table_ref[0] = jnp.broadcast_to(table, grad_table_ref.shape[1:])

    @pl.when(item == 0)
    def _():
        proj_total()

    @pl.when(item > 0)
    def _():
        before[4]()

    count = 3 * hd
    grad_w = nn(grad_ref[0], rows_v[...])
    gain = jnp.sum(w_ref[...].astype(F32) * grad_w, axis=0, keepdims=True)
    gain_ref[0] = jnp.broadcast_to(gain, gain_ref.shape[1:])
    share = hidden // source.shape[2]
    whole = [grad_w.astype(BF16), proj_sum[pl.ds(pl.multiple_of(item * share, share), share), :]]
    size = parts.shape[3]
    if 2 * lines * size > count + share:
        whole.append(jnp.zeros((2 * lines * size - count - share, grad_w.shape[1]), BF16))
    whole = jnp.concatenate(whole, axis=0)
    for p in range(2 * lines):
        parts[item, p // 2, p % 2] = whole[p * size : (p + 1) * size]

    @pl.when(item < heads - 1)
    def _():
        stages(jnp.minimum(item, heads - 2))[0]()

    @pl.when(item == heads - 1)
    def _():
        stores = [
            pltpu.make_async_copy(sums, reduced, load_sem.at[0]),
            pltpu.make_async_copy(parts.at[parts.shape[0] - 1], last, load_sem.at[1]),
        ]
        for store in stores:
            store.start()
        for store in stores:
            store.wait()
        for n in range(source.shape[2]):
            for k in range(seqs):
                origin, target, sent, arrival, to, is_self = piece(k, n)

                @pl.when(jnp.logical_not(is_self))
                def _():
                    remote(origin, target, sent, arrival, to).wait_send()


def attend_backward(
    bucket, strips, qkv_t, out_t, lse, qkv_weight_t, att, grad_branch, proj, normed, buckets, n_head, n_seq, bi=512, bj=1024
):
    heads, hd, qlen = out_t.shape
    own, _, tsd = att.shape
    seqs = qlen // tsd
    length, width = normed.shape
    hidden = heads * hd
    total = 2 * length
    lines = n_seq // 2
    piece = -(-(3 * hd + hidden // heads) // (16 * n_seq)) * 16
    q_spec = pl.BlockSpec((1, hd, qlen), lambda n: (n, 0, 0))
    hbm = pl.BlockSpec(memory_space=pl.ANY)
    return pl.pallas_call(
        functools.partial(backward_kernel, length, qlen, hd, tsd, bi, bj, own, seqs, n_head, buckets),
        grid=(heads,),
        out_shape=[
            jax.ShapeDtypeStruct((heads, 3 * hd, length), BF16),
            jax.ShapeDtypeStruct((heads, 8, 128), F32),
            jax.ShapeDtypeStruct((heads, 8, width), F32),
            jax.ShapeDtypeStruct((heads - 1, lines, 2, piece, width), BF16),
            jax.ShapeDtypeStruct((lines, 2, piece, width), BF16),
        ],
        in_specs=[
            pl.BlockSpec((1, total), lambda n: (0, 0)),
            pl.BlockSpec((1,) + strips.shape[1:], lambda n: (n, 0, 0)),
            pl.BlockSpec((1, 1, hd, length), lambda n: (n, 0, 0, 0)),
            pl.BlockSpec((1, 1, hd, length), lambda n: (n, 1, 0, 0)),
            pl.BlockSpec((1, 1, hd, length), lambda n: (n, 2, 0, 0)),
            q_spec,
            pl.BlockSpec((1, 1, qlen), lambda n: (n, 0, 0)),
            pl.BlockSpec((3 * hd, width), lambda n: (n, 0)),
            hbm,
            hbm,
            hbm,
            hbm,
        ],
        out_specs=[
            pl.BlockSpec((1, 3 * hd, length), lambda n: (n, 0, 0)),
            pl.BlockSpec((1, 8, 128), lambda n: (n, 0, 0)),
            pl.BlockSpec((1, 8, width), lambda n: (n, 0, 0)),
            hbm,
            hbm,
        ],
        scratch_shapes=[
            pltpu.VMEM((own, n_head, heads, hd, tsd), BF16),
            pltpu.VMEM(att.shape, BF16),
            pltpu.VMEM(grad_branch.shape, BF16),
            pltpu.VMEM(proj.shape, BF16),
            pltpu.VMEM((total - 128, 128), F32),
            pltpu.VMEM((4 * hd, length), BF16),
            pltpu.VMEM((qlen, 4 * hd), BF16),
            pltpu.VMEM((2 * hd, length), BF16),
            pltpu.VMEM((qlen, 2 * hd), BF16),
            pltpu.VMEM((hd, qlen), BF16),
            pltpu.VMEM((hd, length), F32),
            pltpu.VMEM((hd, length), F32),
            pltpu.VMEM((heads, hd, qlen), BF16),
            pltpu.VMEM((length, width), BF16),
            pltpu.VMEM((n_head, hidden, width), BF16),
            pltpu.VMEM((2, hidden, width), BF16),
            pltpu.VMEM((hidden, width), BF16),
            pltpu.VMEM((hidden, width), BF16),
            pltpu.VMEM((hidden, width), BF16),
            pltpu.VMEM((heads, lines, 2, piece, width), BF16),
            pltpu.VMEM((heads - 1, lines, piece, width), BF16),
            pltpu.VMEM((heads - 1, lines, piece, width), BF16),
            pltpu.VMEM((heads - 1, lines, piece, width), BF16),
            pltpu.VMEM((heads - 1, piece, width), BF16),
            pltpu.VMEM((heads - 1, lines, 2, piece, width), BF16),
            pltpu.SemaphoreType.DMA((seqs, heads)),
            pltpu.SemaphoreType.DMA((seqs, heads)),
            pltpu.SemaphoreType.DMA((4,)),
            pltpu.SemaphoreType.DMA((3,)),
            pltpu.SemaphoreType.DMA((3,)),
            pltpu.SemaphoreType.DMA((heads - 1, 1 + lines)),
            pltpu.SemaphoreType.DMA((heads - 1, 1 + lines)),
            pltpu.SemaphoreType.DMA((heads - 1, 2, lines)),
            pltpu.SemaphoreType.DMA((heads - 1, 2, lines)),
        ],
        compiler_params=pltpu.CompilerParams(
            collective_id=3, has_side_effects=True, vmem_limit_bytes=62 * MB
        ),
        name="attend_backward",
    )(bucket, strips, qkv_t, qkv_t, qkv_t, out_t, lse, qkv_weight_t, att, grad_branch, proj, normed)


MESH = pl.DeviceIdType.MESH


def greet(peers, wait=True):
    barrier = pltpu.get_barrier_semaphore()
    for peer in peers:
        pl.semaphore_signal(barrier, inc=1, device_id=peer, device_id_type=MESH)
    if wait:
        pl.semaphore_wait(barrier, len(peers))


def remote(source, target, send, recv, peer):
    return pltpu.make_async_remote_copy(
        src_ref=source,
        dst_ref=target,
        send_sem=send,
        recv_sem=recv,
        device_id=peer,
        device_id_type=MESH,
    )


def start_any(source, target, send, recv, peer, is_self):
    @pl.when(is_self)
    def _():
        pltpu.make_async_copy(source, target, recv).start()

    @pl.when(jnp.logical_not(is_self))
    def _():
        remote(source, target, send, recv, peer).start()


def wait_any(source, target, send, recv, peer, is_self):
    remote(source, target, send, recv, peer).wait_recv()

    @pl.when(jnp.logical_not(is_self))
    def _():
        remote(source, target, send, recv, peer).wait_send()


def line_to_batch(line, seqs):
    return line % 2 * (seqs // 2) + line // 2


def batch_to_line(batch, seqs):
    return batch % (seqs // 2) * 2 + batch // (seqs // 2)


def gather_kernel(
    n_seq, ways, seqs, tsd, share, tokens, gain, w_ref, bucket, table, out, qkv_out, strips_f, strips_b,
    rows, qkv, tokens_v, rows_in, strip_v, wide, own_sem, a_send, a_recv, p_send, p_recv, o_sem, s_sem,
):
    head, seq = lax.axis_index("head"), lax.axis_index("seq")
    cross, sibling, beside = (head ^ 2, seq), (head ^ 1, seq), (head, seq ^ 1)
    lines = n_seq // 2
    first = pl.ds(pl.multiple_of(head * share, share), share)
    loads = [
        pltpu.make_async_copy(tokens.at[first], tokens_v.at[first], own_sem.at[0]),
        pltpu.make_async_copy(tokens, tokens_v, own_sem.at[1]),
    ]
    peers = [(head, seq ^ (2 * k)) for k in range(1, lines)] + [cross, sibling, beside]
    loads[0].start()
    greet(peers, wait=False)
    loads[0].wait()
    few = min(share, 64)

    gains = jnp.concatenate([gain[n : n + 1, :] for n in range(gain.shape[0])], axis=1)

    def normed(x):
        return (x * rms_inverse(x) * gains).astype(BF16)

    def part(t, _):
        x = tokens_v[pl.ds(head * share + t * few, few)].astype(F32)
        for n in range(seqs):
            rows_in[n, pl.ds(pl.multiple_of(t * few, few), few), :] = normed(x[:, n])
        return 0

    lax.fori_loop(0, share // few, part, 0)
    loads[1].start()
    pl.semaphore_wait(pltpu.get_barrier_semaphore(), len(peers))

    def share_of(k, of_head, part=None):
        at = (seq ^ k) * tsd + of_head * share
        if part is None:
            return rows.at[pl.ds(pl.multiple_of(at, share), share), :]
        return rows.at[pl.ds(pl.multiple_of(at + part * (share // 2), share // 2), share // 2), :]

    started = []

    def launch(source, target, send_sem, recv_sem, peer):
        copy = remote(source, target, send_sem, recv_sem, peer)
        copy.start()
        started.append(copy)

    def here(of_head):
        at = seq * tsd + of_head * share
        return rows.at[pl.ds(pl.multiple_of(at, share), share), :]

    queue = [k for k in range(1, lines) if k >= lines // 2] + [k for k in range(1, lines) if k < lines // 2]
    queue = queue[:1] + queue[lines // 2 :] + queue[1 : lines // 2]
    flying = []

    def dispatch():
        if queue:
            k = queue.pop(0)
            to = seq ^ (2 * k)
            source = rows_in.at[line_to_batch(lax.div(to, ways), seqs)]
            flying.append(remote(source, here(head), a_send.at[k], a_recv.at[k], (head, to)))
            flying[-1].start()

    order = list(queue)
    order = order[1:2] + order[:1] + order[2:]
    dispatch()
    dispatch()

    batch = line_to_batch(lax.div(seq, ways), seqs)
    loads[1].wait()

    def normalise(t, _):
        at = pl.ds(pl.multiple_of(t * few, few), few)
        all_here = tokens_v[at].astype(F32)
        x = all_here[:, 0]
        for n in range(1, seqs):
            x = jnp.where(batch == n, all_here[:, n], x)
        rows[pl.ds(pl.multiple_of(seq * tsd + t * few, few), few), :] = normed(x)
        return 0

    lax.fori_loop(0, tsd // few, normalise, 0)
    launch(here(head), here(head), p_send.at[1, 1], p_recv.at[1, 1], beside)

    heads = table.shape[0]
    jobs = [(n, kind) for n in range(heads) for kind in range(2)]
    strip_out = {}

    def build():
        if jobs:
            n, kind = jobs.pop(0)
            if kind in strip_out:
                strip_out[kind].wait()
            window = biases(bucket[...], table[n : n + 1, :])
            if kind == 0:
                build_transposed(window, strip_v.at[0], wide)
            else:
                build_strip(window, strip_v.at[1])
            target = (strips_f, strips_b)[kind].at[n]
            strip_out[kind] = pltpu.make_async_copy(strip_v.at[kind], target, s_sem.at[kind])
            strip_out[kind].start()

    def send(kind, k, of_head, peer, to_k=None, part=None):
        ref = share_of(k, of_head, part)
        to_k = k if to_k is None else to_k
        launch(ref, ref, p_send.at[kind, k], p_recv.at[kind, to_k], peer)

    def arrived(kind, k, of_head, part=None):
        ref = share_of(k, of_head, part)
        remote(ref, ref, p_send.at[kind, k], p_recv.at[kind, k], cross).wait_recv()

    def stage_own(k):
        if k:
            ref = share_of(2 * k, head)
            remote(ref, ref, a_send.at[k], a_recv.at[k], cross).wait_recv()
            send(0, 2 * k, head, cross)
            send(1, 2 * k, head, beside, 2 * k + 1)
            send(4, 2 * k, head, sibling)

    def stage_pass(k):
        if k:
            arrived(0, 2 * k, head ^ 2)
            send(2, 2 * k, head ^ 2, beside, 2 * k + 1, 0)
            send(5, 2 * k, head ^ 2, sibling)
        arrived(1, 2 * k + 1, head)
        send(3, 2 * k + 1, head, cross, None, 1 if k else None)
        send(6, 2 * k + 1, head, sibling)

    def stage_last(k):
        if k:
            arrived(2, 2 * k + 1, head ^ 2, 0)
            arrived(3, 2 * k + 1, head ^ 2, 1)
        else:
            arrived(3, 1, head ^ 2)
        send(7, 2 * k + 1, head ^ 2, sibling)

    def project(k, even):
        block = 2 * k + (0 if even else 1)
        if even and block:
            arrived(4, block, head ^ 1)
            arrived(5, block, head ^ 3)
        elif block:
            arrived(6, block, head ^ 1)
            arrived(7, block, head ^ 3)
        at = pl.ds(pl.multiple_of((seq ^ block) * tsd, tsd), tsd)
        qkv[:, at] = nt(w_ref[...], rows[at, :]).astype(BF16)
        for n, (source, target) in enumerate(((rows.at[at, :], out.at[at, :]), (qkv.at[:, at], qkv_out.at[:, at]))):
            copy = pltpu.make_async_copy(source, target, o_sem.at[n, block])
            copy.start()
            stored.append(copy)

    stored = []
    project(0, True)
    build()
    order = [0] + order
    for step in range(len(order) + 2):
        if step < len(order):
            stage_own(order[step])
            if step and queue:
                flying.pop(0).wait_send()
                dispatch()
        if 0 <= step - 1 < len(order):
            stage_pass(order[step - 1])
        if 0 <= step - 2 < len(order):
            stage_last(order[step - 2])
            if order[step - 2]:
                project(order[step - 2], True)
        if 0 <= step - 3 < len(order):
            project(order[step - 3], False)
        build()
    project(order[-1], False)
    for copy in started + flying:
        copy.wait_send()
    while jobs:
        build()
    for copy in stored + list(strip_out.values()):
        copy.wait()


def gather_rows(tokens, gain, qkv_weight_t, bucket, table, n_head, n_seq, ways):
    tsd, seqs, width = tokens.shape
    share = tsd // n_head
    length = n_seq * tsd
    columns = qkv_weight_t.shape[0]
    strips = (table.shape[0], 2 * length - 128, 128)
    hbm = pl.BlockSpec(memory_space=pl.ANY)
    vmem = pl.BlockSpec(memory_space=pltpu.VMEM)
    return pl.pallas_call(
        functools.partial(gather_kernel, n_seq, ways, seqs, tsd, share),
        out_shape=[
            jax.ShapeDtypeStruct((length, width), BF16),
            jax.ShapeDtypeStruct((columns, length), BF16),
            jax.ShapeDtypeStruct(strips, F32),
            jax.ShapeDtypeStruct(strips, F32),
        ],
        in_specs=[hbm, vmem, vmem, vmem, vmem],
        out_specs=[hbm] * 4,
        scratch_shapes=[
            pltpu.VMEM((length, width), BF16),
            pltpu.VMEM((columns, length), BF16),
            pltpu.VMEM(tokens.shape, BF16),
            pltpu.VMEM((seqs, share, width), BF16),
            pltpu.VMEM((2,) + strips[1:], F32),
            pltpu.VMEM((128, 2 * length), F32),
            pltpu.SemaphoreType.DMA((2,)),
            pltpu.SemaphoreType.DMA((n_seq // 2,)),
            pltpu.SemaphoreType.DMA((n_seq // 2,)),
            pltpu.SemaphoreType.DMA((8, n_seq)),
            pltpu.SemaphoreType.DMA((8, n_seq)),
            pltpu.SemaphoreType.DMA((2, n_seq)),
            pltpu.SemaphoreType.DMA((2,)),
        ],
        compiler_params=pltpu.CompilerParams(
            collective_id=1, has_side_effects=True, vmem_limit_bytes=60 * MB
        ),
        name="gather_rows",
    )(tokens, gain, qkv_weight_t, bucket, table)


def to_residual_kernel(own, ways, seqs, n_head, tsd, source, proj, out, proj_out, send, recv, p_sem, p_send, p_recv):
    head, seq = lax.axis_index("head"), lax.axis_index("seq")
    batch, half = line_to_batch(lax.div(seq, ways), seqs), lax.rem(seq, ways)
    to_head = lax.div(batch, own)
    inner = lax.rem(batch, own)
    mine_half = lax.rem(seq, ways)
    mine_at = lax.div(seq, ways)
    sibling, cross = (head ^ 1, seq), (head ^ 2, seq)
    greet_both(own, ways, seqs, n_head, head, seq, (sibling, cross))
    kept = pltpu.make_async_copy(proj, proj_out.at[head], p_sem)
    kept.start()
    moves = [
        remote(proj, proj_out.at[head], p_send.at[0], p_recv.at[0], cross),
        remote(proj, proj_out.at[head], p_send.at[1], p_recv.at[1], sibling),
    ]
    for move in moves:
        move.start()
    calls = []
    for k in range(seqs):
        j = lax.rem(head * own + inner + k, seqs)
        to_seq = j * ways + half
        is_self = jnp.logical_and(to_head == head, to_seq == seq)
        piece = source.at[:, pl.ds(pl.multiple_of(j * tsd, tsd), tsd)]
        args = (piece, out.at[inner, head], send.at[k], recv.at[k], (to_head, to_seq), is_self)
        start_any(*args)
        calls.append(args)
    passed = proj_out.at[head ^ 2]
    remote(passed, passed, p_send.at[0], p_recv.at[0], cross).wait_recv()
    moves.append(remote(passed, passed, p_send.at[2], p_recv.at[2], sibling))
    moves[2].start()
    for n, of in ((1, head ^ 1), (2, head ^ 3)):
        landed = proj_out.at[of]
        remote(landed, landed, p_send.at[n], p_recv.at[n], sibling).wait_recv()
    for move in moves:
        move.wait_send()
    kept.wait()
    for k, args in enumerate(calls):
        number = lax.rem(mine_at - k + seqs, seqs)
        from_head, from_inner = lax.div(number, own), lax.rem(number, own)
        landed = out.at[from_inner, from_head]
        remote(landed, landed, send.at[k], recv.at[k], (to_head, seq)).wait_recv()
        piece, target, sem, arrival, peer, is_self = args

        @pl.when(jnp.logical_not(is_self))
        def _():
            remote(piece, target, sem, arrival, peer).wait_send()


def greet_both(own, ways, seqs, n_head, head, seq, others=(), wait=True):
    batch, half = line_to_batch(lax.div(seq, ways), seqs), lax.rem(seq, ways)
    inner = lax.rem(batch, own)
    mine_half, mine_at = lax.rem(seq, ways), lax.div(seq, ways)
    barrier = pltpu.get_barrier_semaphore()
    for k in range(seqs):
        j = lax.rem(head * own + inner + k, seqs)
        number = lax.rem(mine_at - k + seqs, seqs)
        source_seq = batch_to_line(head * own + lax.rem(number, own), seqs) * ways + mine_half
        for peer in ((lax.div(batch, own), j * ways + half), (lax.div(number, own), source_seq)):
            pl.semaphore_signal(barrier, inc=1, device_id=peer, device_id_type=MESH)
    for peer in others:
        pl.semaphore_signal(barrier, inc=1, device_id=peer, device_id_type=MESH)
    if wait:
        pl.semaphore_wait(barrier, 2 * seqs + len(others))


def to_residual(source, proj, own, ways, seqs, n_head, tsd):
    rows = source.shape[0]
    hbm = pl.BlockSpec(memory_space=pl.ANY)
    return pl.pallas_call(
        functools.partial(to_residual_kernel, own, ways, seqs, n_head, tsd),
        out_shape=[
            jax.ShapeDtypeStruct((own, n_head, rows, tsd), BF16),
            jax.ShapeDtypeStruct((n_head,) + proj.shape, BF16),
        ],
        in_specs=[hbm, hbm],
        out_specs=[hbm, hbm],
        scratch_shapes=[
            pltpu.SemaphoreType.DMA((seqs,)),
            pltpu.SemaphoreType.DMA((seqs,)),
            pltpu.SemaphoreType.DMA,
            pltpu.SemaphoreType.DMA((3,)),
            pltpu.SemaphoreType.DMA((3,)),
        ],
        compiler_params=pltpu.CompilerParams(collective_id=2, has_side_effects=True),
        name="to_residual",
    )(source, proj)


SQRT_2_PI = math.sqrt(2.0 / math.pi)


def tn(a, b):
    return lax.dot_general(a, b, (((0,), (0,)), ((), ())), preferred_element_type=F32)


def experts_kernel(
    n_head, n_seq, mains, tails, tile,
    sending, w_in, w_out, back, rows_out, grads_out, act_out, pre_out,
    got, ret, v_in, v_out, rows_all, grads_all, act_all, pre_all,
    send, recv, r_send, r_recv, w_sem, o_sem,
):
    width, hidden = v_in.shape
    devices = n_head * n_seq
    me = lax.axis_index("head") * n_seq + lax.axis_index("seq")
    group = 8
    count = group * (16 * mains + 8 * tails)
    fold = width // 2
    base = mains * 2 * width

    def place(k):
        other = me ^ k
        return lax.div(other, n_seq), lax.rem(other, n_seq)

    barrier = pltpu.get_barrier_semaphore()

    def signal(k, _):
        pl.semaphore_signal(barrier, inc=1, device_id=place(k), device_id_type=MESH)
        return 0

    lax.fori_loop(1, devices, signal, 0)
    load_in = pltpu.make_async_copy(w_in, v_in, w_sem.at[0])
    load_out = pltpu.make_async_copy(w_out, v_out, w_sem.at[1])
    load_in.start()
    load_out.start()
    pl.semaphore_wait(barrier, devices - 1)
    mine = pltpu.make_async_copy(sending.at[me], got.at[me], recv.at[0])
    mine.start()

    def dispatch(k, _):
        remote(sending.at[me ^ k], got.at[me], send.at[k], recv.at[k], place(k)).start()
        return 0

    lax.fori_loop(1, devices, dispatch, 0)
    load_in.wait()
    load_out.wait()
    low = lax.broadcasted_iota(jnp.int32, (8, width), 0) < 4

    def chunk(c, _):
        first = c * count

        @pl.when(c == 0)
        def _():
            mine.wait()

        for i in range(group):
            k = c * group + i

            @pl.when(k > 0)
            def _():
                landed = got.at[me ^ k]
                remote(landed, landed, send.at[k], recv.at[k], place(k)).wait_recv()

        for i in range(group):
            source = me ^ (c * group + i)
            for j in range(mains):
                at = pl.ds(pl.multiple_of(first + (j * group + i) * 16, 16), 16)
                rows_all[at, :] = got[source, :, j * 2 * width : j * 2 * width + width]
                grads_all[at, :] = got[source, :, j * 2 * width + width : (j + 1) * 2 * width]
        for u in range(tails):
            for i in range(0, group, 2):
                rows, grads = [], []
                for n in range(2):
                    folded = got[me ^ (c * group + i + n), :, base + u * fold : base + (u + 1) * fold].astype(F32)
                    wide = jnp.concatenate([folded[:8], folded[8:]], axis=1)
                    rows.append(jnp.where(low, wide, 0.0))
                    grads.append(jnp.where(low, pltpu.roll(wide, 4, 0), 0.0))
                at = pl.ds(pl.multiple_of(first + mains * group * 16 + u * group * 8 + i * 8, 16), 16)
                rows_all[at, :] = jnp.concatenate(rows, axis=0).astype(BF16)
                grads_all[at, :] = jnp.concatenate(grads, axis=0).astype(BF16)
        here = pl.ds(pl.multiple_of(first, 16), count)
        x, d = rows_all[here, :], grads_all[here, :]

        def slab(t, carry):
            result, slots = carry
            columns = pl.ds(pl.multiple_of(t * tile, tile), tile)
            pre = nn(x, v_in[:, columns])
            square = pre * pre
            t_value = jnp.tanh(SQRT_2_PI * pre * (1.0 + 0.044715 * square))
            cdf = 0.5 * (1.0 + t_value)
            act = (pre * cdf).astype(BF16)
            slope = cdf + 0.5 * pre * (1.0 - t_value * t_value) * (SQRT_2_PI * (1.0 + 0.134145 * square))
            grad_pre = (nt(d, v_out[columns, :]) * slope).astype(BF16)
            act_all[here, columns] = act
            pre_all[here, columns] = grad_pre
            return result + nn(act, v_out[columns, :]), slots + nt(grad_pre, v_in[:, columns])

        zero = jnp.zeros((count, width), F32)
        result, slots = lax.fori_loop(0, hidden // tile, slab, (zero, zero))
        for i in range(group):
            source = me ^ (c * group + i)
            for j in range(mains):
                at = (j * group + i) * 16
                ret[source, :, j * 2 * width : j * 2 * width + width] = result[at : at + 16].astype(BF16)
                ret[source, :, j * 2 * width + width : (j + 1) * 2 * width] = slots[at : at + 16].astype(BF16)
            for u in range(tails):
                at = mains * group * 16 + u * group * 8 + i * 8
                wide = jnp.where(low, result[at : at + 8], pltpu.roll(slots[at : at + 8], 4, 0))
                folded = jnp.concatenate([wide[:, :fold], wide[:, fold:]], axis=0)
                ret[source, :, base + u * fold : base + (u + 1) * fold] = folded.astype(BF16)
        for i in range(group):
            k = c * group + i

            @pl.when(k == 0)
            def _():
                pltpu.make_async_copy(ret.at[me], back.at[me], r_recv.at[0]).start()

            @pl.when(k > 0)
            def _():
                remote(ret.at[me ^ k], back.at[me], r_send.at[k], r_recv.at[k], place(k)).start()

        return 0

    lax.fori_loop(0, devices // group, chunk, 0)

    kept = []
    for n, (source, target) in enumerate(
        ((rows_all, rows_out), (grads_all, grads_out), (act_all, act_out), (pre_all, pre_out))
    ):
        copy = pltpu.make_async_copy(source, target, o_sem.at[n])
        copy.start()
        kept.append(copy)
    for copy in kept:
        copy.wait()
    pltpu.make_async_copy(ret.at[me], back.at[me], r_recv.at[0]).wait()

    def finish(k, _):
        landed = back.at[me ^ k]
        remote(landed, landed, r_send.at[k], r_recv.at[k], place(k)).wait()
        remote(landed, landed, send.at[k], recv.at[k], place(k)).wait_send()
        return 0

    lax.fori_loop(1, devices, finish, 0)


def run_experts(sending, expert_in, expert_out, n_head, n_seq, mains, tails):
    devices = n_head * n_seq
    width, hidden = expert_in.shape
    rows = devices * (16 * mains + 8 * tails)
    tile = width
    hbm = pl.BlockSpec(memory_space=pl.ANY)
    return pl.pallas_call(
        functools.partial(experts_kernel, n_head, n_seq, mains, tails, tile),
        out_shape=[
            jax.ShapeDtypeStruct(sending.shape, BF16),
            jax.ShapeDtypeStruct((rows, width), BF16),
            jax.ShapeDtypeStruct((rows, width), BF16),
            jax.ShapeDtypeStruct((rows, hidden), BF16),
            jax.ShapeDtypeStruct((rows, hidden), BF16),
        ],
        in_specs=[hbm] * 3,
        out_specs=[hbm] * 5,
        scratch_shapes=[
            pltpu.VMEM(sending.shape, BF16),
            pltpu.VMEM(sending.shape, BF16),
            pltpu.VMEM((width, hidden), BF16),
            pltpu.VMEM((hidden, width), BF16),
            pltpu.VMEM((rows, width), BF16),
            pltpu.VMEM((rows, width), BF16),
            pltpu.VMEM((rows, hidden), BF16),
            pltpu.VMEM((rows, hidden), BF16),
            pltpu.SemaphoreType.DMA((devices,)),
            pltpu.SemaphoreType.DMA((devices,)),
            pltpu.SemaphoreType.DMA((devices,)),
            pltpu.SemaphoreType.DMA((devices,)),
            pltpu.SemaphoreType.DMA((2,)),
            pltpu.SemaphoreType.DMA((4,)),
        ],
        compiler_params=pltpu.CompilerParams(
            collective_id=4, has_side_effects=True, vmem_limit_bytes=60 * MB
        ),
        name="run_experts",
    )(sending, expert_in, expert_out)


def weights_kernel(rows_ref, grads_ref, act_ref, pre_ref, g_in_ref, g_out_ref):
    g_out_ref[...] = tn(act_ref[...], grads_ref[...])
    g_in_ref[...] = tn(rows_ref[...], pre_ref[...])


def expert_weights(rows, grads, act, pre):
    count, width = rows.shape
    hidden = act.shape[1]
    tile = width
    whole = pl.BlockSpec((count, width), lambda t: (0, 0))
    column = pl.BlockSpec((count, tile), lambda t: (0, t))
    return pl.pallas_call(
        weights_kernel,
        grid=(hidden // tile,),
        out_shape=[jax.ShapeDtypeStruct((width, hidden), F32), jax.ShapeDtypeStruct((hidden, width), F32)],
        in_specs=[whole, whole, column, column],
        out_specs=[pl.BlockSpec((width, tile), lambda t: (0, t)), pl.BlockSpec((tile, width), lambda t: (t, 0))],
        compiler_params=pltpu.CompilerParams(vmem_limit_bytes=48 * MB),
        cost_estimate=pl.CostEstimate(
            flops=4 * count * width * hidden, bytes_accessed=12 * width * hidden, transcendentals=0
        ),
        name="expert_weights",
    )(rows, grads, act, pre)


def finish_kernel(
    n_head, n_seq, ways, groups,
    buckets, grads, w_ref, weights, small_ref, gains, tables, out, weights_out, small_out,
    small, sent1, mine, got1, got2, got3, sum1, sum2, got_w, sum_w, got_z, own_w, got_near, sum_near, got_far, own_small, all_small,
    send, recv, y_send, y_recv, z_send, z_recv, near_sends, near_recvs, far_sends, far_recvs,
):
    head, seq = lax.axis_index("head"), lax.axis_index("seq")
    core, x = lax.rem(head, 2), lax.div(head, 2)
    y = lax.rem(seq, ways)
    sibling, cross, beside = (head ^ 1, seq), (head ^ 2, seq), (head, seq ^ 1)
    line, lines = lax.div(seq, 2), n_seq // 2
    side = x ^ lax.rem(lax.div(line, 2), 2)
    length = grads.shape[1]
    tsd = length // n_seq
    rows = tsd // 2

    near = [(head ^ (k // 2), seq ^ (k % 2)) for k in range(1, 2 * n_head)]
    far = [(head, seq ^ (2 * k)) for k in range(1, lines)]
    greet(near + far, wait=False)
    small[...] = small_ref[...]
    width = w_ref.shape[1]
    chunks = width // 128
    extra = 8 - chunks
    gain = functools.reduce(jnp.add, [gains[n, :1, :] for n in range(gains.shape[0])])
    for n in range(chunks):
        tile, row = (chunks + n) // extra, chunks + (chunks + n) % extra
        small[tile // n_seq, tile % n_seq // 2, tile % 2, row : row + 1, :] = gain[:, n * 128 : (n + 1) * 128]
    rows_of = [tables[n, :1, :buckets] for n in range(tables.shape[0])]
    rows_of.append(jnp.zeros((1, 128 - buckets * len(rows_of)), F32))
    tile = 8 + head
    small[lax.div(tile, n_seq), lax.div(lax.rem(tile, n_seq), 2), lax.rem(tile, 2), chunks : chunks + 1, :] = (
        jnp.concatenate(rows_of, axis=1)
    )
    waits = []

    def go(source, target, send_sem, recv_sem, peer):
        copy = remote(source, target, send_sem, recv_sem, peer)
        copy.start()
        waits.append(copy)

    def landed(target, send_sem, recv_sem, peer=sibling):
        remote(target, target, send_sem, recv_sem, peer).wait_recv()

    first, second_w, third, fourth, fifth = sum_over_seq(
        head, seq, weights, got_w, sum_w, got_z, own_w, weights_out, y_send, y_recv, z_send, z_recv
    )
    order = [(1, 1), (1, 0), (0, 1), (0, 0)]

    def grad_rows(of_core, v, dx, dy):
        block = of_core * 4 * groups + v * 4 + (side ^ dx) * 2 + (y ^ dy)
        at = pl.ds(pl.multiple_of(block * tsd, tsd), tsd)
        return tn(grads[:, at], w_ref[...])

    def pass_on(v, b):
        dx, dy = order[b]
        landed(got1.at[v, b], send.at[0, v, b], recv.at[0, v, b])
        total = (mine[v, b] + got1[v, b].astype(F32)).astype(BF16)
        sum1[v, b, 0] = total[:rows]
        sum1[v, b, 1] = total[rows:]
        if dx == 1:
            to = 1 - dy
            go(sum1.at[v, b, 0], got2.at[v, to], send.at[1, v, to], recv.at[1, v, to], cross)
        if dy == 1:
            to = 3 - dx
            go(sum1.at[v, b, 1], got2.at[v, to], send.at[1, v, to], recv.at[1, v, to], beside)

    pair = lax.rem(seq, 2)
    before = None
    for v in range(groups):
        for b, (dx, dy) in enumerate(order):
            sent1[v, b] = grad_rows(1 - core, v, dx, dy).astype(BF16)
            if before is None:
                pl.semaphore_wait(pltpu.get_barrier_semaphore(), len(near) + len(far))
                for k, peer in enumerate(near, 1):
                    part = small.at[head ^ (k // 2), :, pair ^ (k % 2)]
                    go(part, got_near.at[k], near_sends.at[0, k], near_recvs.at[0, k], peer)
            go(sent1.at[v, b], got1.at[v, b], send.at[0, v, b], recv.at[0, v, b], sibling)
            mine[v, b] = grad_rows(core, v, dx, dy)
            if before is None:
                first()
            if before is not None:
                pass_on(*before)
            before = (v, b)
    pass_on(*before)

    kept = {
        0: (order.index((0, 1)), 0),
        1: (order.index((0, 0)), 0),
        2: (order.index((1, 0)), 1),
        3: (order.index((0, 0)), 1),
    }

    def second(v, slot):
        landed(got2.at[v, slot], send.at[1, v, slot], recv.at[1, v, slot])
        b, w = kept[slot]
        sum2[v, slot] = (sum1[v, b, w].astype(F32) + got2[v, slot].astype(F32)).astype(BF16)
        if slot == 0:
            go(sum2.at[v, 0], got3.at[v, 0], send.at[2, v, 0], recv.at[2, v, 0], beside)
        if slot == 2:
            go(sum2.at[v, 2], got3.at[v, 1], send.at[2, v, 1], recv.at[2, v, 1], cross)

    total = small[head, :, pair]
    for k in range(1, 2 * n_head):
        landed(got_near.at[k], near_sends.at[0, k], near_recvs.at[0, k])
        total = total + got_near[k]
    sum_near[...] = total
    for k, peer in enumerate(far, 1):
        go(sum_near.at[line ^ k], got_far.at[k], far_sends.at[0, k], far_recvs.at[0, k], peer)
    second_w()
    total = sum_near[line]
    for k in range(1, lines):
        landed(got_far.at[k], far_sends.at[0, k], far_recvs.at[0, k])
        total = total + got_far[k]
    own_small[...] = total
    all_small[line] = total
    for k, peer in enumerate(far, 1):
        go(own_small, all_small.at[line], far_sends.at[1, k], far_recvs.at[1, k], peer)
    for v in range(groups):
        second(v, 0)
    for k in range(1, lines):
        landed(all_small.at[line ^ k], far_sends.at[1, k], far_recvs.at[1, k])
    small_out[head, :, pair] = all_small[...]
    for k, peer in enumerate(near, 1):
        go(all_small, small_out.at[head, :, pair], near_sends.at[1, k], near_recvs.at[1, k], peer)
    for v in range(groups):
        second(v, 2)
    third()
    for slot in (1, 3):
        for v in range(groups):
            second(v, slot)
    fourth()
    for w in (1, 0):
        for v in range(groups):
            landed(got3.at[v, w], send.at[2, v, w], recv.at[2, v, w])
            out[v, w] = (sum2[v, 1 + 2 * w].astype(F32) + got3[v, w].astype(F32)).astype(BF16)
    for k in range(1, 2 * n_head):
        part = small_out.at[head ^ (k // 2), :, pair ^ (k % 2)]
        landed(part, near_sends.at[1, k], near_recvs.at[1, k])
    fifth()
    for copy in waits:
        copy.wait_send()


def finish_sums(grads, qkv_weight_t, weights, small, gains, tables, buckets, n_head, n_seq, ways):
    length = grads.shape[1]
    width = qkv_weight_t.shape[1]
    tsd = length // n_seq
    groups = n_seq // 8
    rows = tsd // 2
    lines, _, piece, _ = weights.shape
    vmem = pl.BlockSpec(memory_space=pltpu.VMEM)
    out, weights, small = pl.pallas_call(
        functools.partial(finish_kernel, n_head, n_seq, ways, groups, buckets),
        out_shape=[
            jax.ShapeDtypeStruct((groups, 2, rows, width), BF16),
            jax.ShapeDtypeStruct(weights.shape, BF16),
            jax.ShapeDtypeStruct((n_head, lines, 2, 8, 128), F32),
        ],
        in_specs=[vmem] * 6,
        out_specs=[vmem] * 3,
        scratch_shapes=[
            pltpu.VMEM((n_head, lines, 2, 8, 128), F32),
            pltpu.VMEM((groups, 4, tsd, width), BF16),
            pltpu.VMEM((groups, 4, tsd, width), F32),
            pltpu.VMEM((groups, 4, tsd, width), BF16),
            pltpu.VMEM((groups, 4, rows, width), BF16),
            pltpu.VMEM((groups, 2, rows, width), BF16),
            pltpu.VMEM((groups, 4, 2, rows, width), BF16),
            pltpu.VMEM((groups, 4, rows, width), BF16),
            pltpu.VMEM((lines, piece, width), BF16),
            pltpu.VMEM((lines, piece, width), BF16),
            pltpu.VMEM((lines, piece, width), BF16),
            pltpu.VMEM((piece, width), BF16),
            pltpu.VMEM((2 * n_head, lines, 8, 128), F32),
            pltpu.VMEM((lines, 8, 128), F32),
            pltpu.VMEM((lines, 8, 128), F32),
            pltpu.VMEM((8, 128), F32),
            pltpu.VMEM((lines, 8, 128), F32),
            pltpu.SemaphoreType.DMA((3, groups, 4)),
            pltpu.SemaphoreType.DMA((3, groups, 4)),
            pltpu.SemaphoreType.DMA((1 + lines,)),
            pltpu.SemaphoreType.DMA((1 + lines,)),
            pltpu.SemaphoreType.DMA((2, lines)),
            pltpu.SemaphoreType.DMA((2, lines)),
            pltpu.SemaphoreType.DMA((2, 2 * n_head)),
            pltpu.SemaphoreType.DMA((2, 2 * n_head)),
            pltpu.SemaphoreType.DMA((2, lines)),
            pltpu.SemaphoreType.DMA((2, lines)),
        ],
        compiler_params=pltpu.CompilerParams(
            collective_id=6, has_side_effects=True, vmem_limit_bytes=56 * MB
        ),
        name="finish_sums",
    )(grads, qkv_weight_t, weights, small.reshape(n_head, lines, 2, 8, 128), gains, tables)
    return out.reshape(groups, tsd, width), weights, small.reshape(n_head * n_seq, 8, 128)


def send_home(blocks, own, seqs, n_head, n_seq):
    groups = blocks.shape[0]
    assert groups == own
    head, seq = lax.axis_index("head"), lax.axis_index("seq")
    inner = line_to_batch(seq // 2, seqs) % own
    rounds = []
    for k in range(own):
        pairs = []
        for a in range(n_head):
            for q in range(n_seq):
                line, y, x, core = q // 2, q % 2, a // 2, a % 2
                batch = line_to_batch(line, seqs)
                v = (k + batch % own) % groups
                home = core * 4 * groups + v * 4 + (x ^ (line // 2 % 2)) * 2 + y
                pairs.append((a * n_seq + q, batch // own * n_seq + home))
        piece = lax.dynamic_index_in_dim(blocks, (k + inner) % groups, 0, keepdims=False) if own > 1 else blocks[0]
        rounds.append(lax.ppermute(piece, ("head", "seq"), pairs))
    if own == 1:
        return rounds[0][None]
    rounds = jnp.stack(rounds)
    at = seq // 4 % groups
    return jnp.stack([lax.dynamic_index_in_dim(rounds, (at - i) % own, 0, keepdims=False) for i in range(own)])


def outputs_kernel(
    columns, n_seq, first_ref, last_ref, small, gain, qkv_ref, proj_ref, router_ref, ffn_ref, attn_ref, bias_ref, table_ref
):
    heads = first_ref.shape[0] + 1
    share = proj_ref.shape[0] // heads
    for n in range(heads):
        rows = last_ref[...] if n == heads - 1 else first_ref[n]
        qkv_ref[n * columns : (n + 1) * columns] = rows[:columns].astype(F32)
        proj_ref[n * share : (n + 1) * share] = rows[columns : columns + share].astype(F32)
    chunks = gain.shape[0]
    extra = 8 - chunks
    for n in range(chunks):
        router_ref[:, n * 128 : (n + 1) * 128] = small[:, n, :]
        ffn_ref[n : n + 1, :] = small[n // extra, chunks + n % extra : chunks + n % extra + 1, :]
        at = chunks + n
        row = small[at // extra, chunks + at % extra : chunks + at % extra + 1, :]
        attn_ref[n : n + 1, :] = row / gain[n : n + 1, :]
    at = 2 * chunks // extra
    bias_ref[...] = small[at, chunks : chunks + 1, :]
    table_ref[...] = small[8 + lax.axis_index("head"), chunks : chunks + 1, :]


def outputs(first, last, small, gain, columns, hidden, n_seq):
    heads, width = first.shape[0] + 1, first.shape[-1]
    assert 2 * (width // 128) % (8 - width // 128) == 0
    vmem = pl.BlockSpec(memory_space=pltpu.VMEM)
    return pl.pallas_call(
        functools.partial(outputs_kernel, columns, n_seq),
        out_shape=[
            jax.ShapeDtypeStruct((heads * columns, width), F32),
            jax.ShapeDtypeStruct((hidden, width), F32),
            jax.ShapeDtypeStruct((small.shape[0], width), F32),
            jax.ShapeDtypeStruct(gain.shape, F32),
            jax.ShapeDtypeStruct(gain.shape, F32),
            jax.ShapeDtypeStruct((1, 128), F32),
            jax.ShapeDtypeStruct((1, 128), F32),
        ],
        in_specs=[vmem] * 4,
        out_specs=[vmem] * 7,
        compiler_params=pltpu.CompilerParams(vmem_limit_bytes=32 * MB),
        name="outputs",
    )(first.reshape(heads - 1, -1, width), last.reshape(-1, width), small, gain)


def last_kernel(sum_ref, x_ref, mid_ref, gain, out_ref):
    gains = jnp.concatenate([gain[n : n + 1, :] for n in range(gain.shape[0])], axis=1)
    x = x_ref[...]
    inverse = rms_inverse(x)
    unit = x * inverse
    scaled = sum_ref[...].astype(F32) * gains
    inner = jnp.mean(scaled * unit, axis=-1, keepdims=True)
    out_ref[...] = (mid_ref[...] + inverse * (scaled - unit * inner)).astype(BF16)


def last_step(sums, x, mid, gain):
    rows, width = x.shape
    block = pl.BlockSpec((rows // 4, width), lambda t: (t, 0))
    return pl.pallas_call(
        last_kernel,
        grid=(4,),
        out_shape=jax.ShapeDtypeStruct((rows, width), BF16),
        in_specs=[block, block, block, pl.BlockSpec(gain.shape, lambda t: (0, 0))],
        out_specs=block,
        compiler_params=pltpu.CompilerParams(vmem_limit_bytes=32 * MB),
        name="last_step",
    )(sums, x, mid, gain)


def rms_inverse(values):
    return lax.rsqrt(jnp.mean(values * values, axis=-1, keepdims=True) + eps)


def dot(a, b, dims, precision=None):
    return lax.dot_general(a, b, (dims, ((), ())), preferred_element_type=F32, precision=precision)


def local(
    n_head,
    n_seq,
    tokens,
    attn_gain,
    qkv_weight,
    bias_table,
    proj_weight,
    ffn_gain,
    router_weight,
    router_bias,
    expert_in,
    expert_out,
    bucket,
    expert_choice,
    priority,
    out_grad,
):
    tsd, seqs, width = tokens.shape
    buckets, heads_here = bias_table.shape
    head_dim = qkv_weight.shape[1] // (3 * heads_here)
    hidden = heads_here * head_dim
    length = bucket.shape[0] // 2
    own = out_grad.shape[1]
    ways = n_seq // seqs
    qlen = length // ways
    experts = router_weight.shape[1]
    devices = n_head * n_seq
    assert ways == 2 and n_head == 4 and own * n_head == seqs and experts == devices
    seq_index = lax.axis_index("seq")
    head_index = lax.axis_index("head")
    half = seq_index % ways

    qkv_weight_t = qkv_weight.T
    offsets = bucket[None, :]
    normed1, qkv_t, strips_f, strips_b = gather_rows(
        tokens, attn_gain.reshape(width // 128, 128), qkv_weight_t, offsets, bias_table.T, n_head, n_seq, ways
    )
    qkv_t = qkv_t.reshape(heads_here, 3, head_dim, length)

    half_at = half.reshape(1)
    attended_t, lse = attend_forward(half_at, strips_f, qkv_t, qlen, tsd)

    spread, proj_full = to_residual(
        attended_t.reshape(hidden, qlen), proj_weight, own, ways, seqs, n_head, tsd
    )
    proj_full = proj_full.reshape(n_head * hidden, width)
    att_all = spread.reshape(own, n_head * hidden, tsd)
    branch = jnp.einsum("bcp,cd->bpd", att_all, proj_full, preferred_element_type=F32)
    rows = own * tsd
    x_own = lax.dynamic_slice_in_dim(tokens, head_index * own, own, 1).astype(F32)
    x_own = jnp.moveaxis(x_own, 1, 0).reshape(rows, width)
    mid = x_own + branch.reshape(rows, width)
    inv2 = rms_inverse(mid)
    normed2 = (mid * inv2 * ffn_gain).astype(BF16)
    logits = dot(normed2, router_weight, ((1,), (0,))) + router_bias
    gates = jax.nn.softmax(logits, axis=1)
    route = expert_choice.T.reshape(rows)
    order = priority.T.reshape(rows)
    same = (route[:, None] == route[None, :]) & (order[None, :] < order[:, None])
    rank = jnp.sum(same.astype(jnp.int32), axis=1)
    capacity = max(2, (5 * rows + 4 * experts - 1) // (4 * experts))
    mains = capacity // 16
    tails = -(-(capacity - 16 * mains) // 4)
    keep = rank < capacity
    chosen = (route[:, None] == jnp.arange(experts, dtype=jnp.int32)[None, :]).astype(F32)
    gate = jnp.sum(gates * chosen, axis=1)
    upstream = jnp.moveaxis(out_grad, 1, 0).astype(F32).reshape(rows, width)
    grad_rows = (gate[:, None] * upstream).astype(BF16)
    beside = jnp.concatenate([normed2, grad_rows], axis=1)
    below = jnp.concatenate([normed2, grad_rows], axis=0)
    fold = width // 2
    placing_mains, placing_tails, sending = [], [], []
    for j in range(mains):
        at = jnp.where(keep & (rank // 16 == j), route * 16 + rank % 16, -1)
        placing = (at[None, :] == jnp.arange(experts * 16, dtype=jnp.int32)[:, None]).astype(BF16)
        placing_mains.append(placing)
        sending.append(dot(placing, beside, ((1,), (0,))).astype(BF16).reshape(experts, 16, 2 * width))
    for u in range(tails):
        from_rank = rank - 16 * mains - 4 * u
        at = jnp.where(keep & (from_rank >= 0) & (from_rank < 4), route * 16 + from_rank, -1)
        at = jnp.concatenate([at, jnp.where(at >= 0, at + 4, -1)])
        lines = jnp.arange(experts * 16, dtype=jnp.int32)[:, None]
        left, right = (at[None, :] == lines).astype(BF16), (at[None, :] + 8 * (at[None, :] >= 0) == lines).astype(BF16)
        placing_tails.append((left, right))
        tail = dot(left, below[:, :fold], ((1,), (0,))) + dot(right, below[:, fold:], ((1,), (0,)))
        sending.append(tail.astype(BF16).reshape(experts, 16, fold))
    back, *kept = run_experts(
        jnp.concatenate(sending, axis=2), expert_in[0], expert_out[0], n_head, n_seq, mains, tails
    )
    grad_expert_in, grad_expert_out = expert_weights(*kept)
    grad_expert_in, grad_expert_out = grad_expert_in[None], grad_expert_out[None]
    expert_rows, grad_disp = 0.0, 0.0
    for j, placing in enumerate(placing_mains):
        main = back[:, :, j * 2 * width : (j + 1) * 2 * width].reshape(experts * 16, 2 * width)
        main = dot(placing, main, ((0,), (0,)))
        expert_rows, grad_disp = expert_rows + main[:, :width], grad_disp + main[:, width:]
    for u, halves in enumerate(placing_tails):
        at = mains * 2 * width + u * fold
        tail = back[:, :, at : at + fold].reshape(experts * 16, fold)
        tail = jnp.concatenate([dot(placing, tail, ((0,), (0,))) for placing in halves], axis=1)
        expert_rows, grad_disp = expert_rows + tail[:rows], grad_disp + tail[rows:]

    output = mid + gate[:, None] * expert_rows
    output = jnp.moveaxis(output.astype(BF16).reshape(own, tsd, width), 0, 1)
    grad_gate = jnp.sum(upstream * expert_rows, axis=1)
    grad_logits = gates * (chosen - gate[:, None]) * grad_gate[:, None]
    grad_router_bias = jnp.sum(grad_logits, axis=0)
    grad_normed2 = grad_disp + dot(grad_logits, router_weight.astype(F32), ((1,), (1,)), HIGH)
    scaled2 = grad_normed2 * ffn_gain
    unit2 = mid * inv2
    grad_ffn_gain = jnp.sum(grad_normed2 * unit2, axis=0)
    grad_mid = upstream + inv2 * (scaled2 - unit2 * jnp.mean(scaled2 * unit2, axis=-1, keepdims=True))
    grad_branch = grad_mid.astype(BF16).reshape(own, tsd, width)

    grad_qkv_t, grad_table, gain_parts, weights_first, weights_last = attend_backward(
        offsets, strips_b, qkv_t, attended_t, lse, qkv_weight_t, att_all, grad_branch, proj_full, normed1, buckets,
        n_head, n_seq,
    )
    grad_qkv_t = grad_qkv_t.reshape(3 * hidden, length)

    late_logits, late_rows, gain_parts = lax.optimization_barrier((grad_logits, normed2, gain_parts))
    grad_router_t = dot(late_logits, late_rows.astype(F32), ((0,), (0,)), HIGH)
    extras = jnp.concatenate([grad_ffn_gain, jnp.zeros((width,), F32), grad_router_bias])
    assert devices >= 8 + n_head and buckets * heads_here <= 128 and 2 * width + experts <= 8 * 256
    lanes = 128
    chunks = width // lanes
    extras = jnp.pad(extras, (0, devices * (8 - chunks) * lanes - extras.shape[0]))
    small = jnp.concatenate(
        [grad_router_t.reshape(experts, chunks, lanes), extras.reshape(devices, 8 - chunks, lanes)], axis=1
    )
    grad_normed1_own, weights_last, small = finish_sums(
        grad_qkv_t, qkv_weight_t, weights_last, small, gain_parts, grad_table, buckets, n_head, n_seq, ways
    )
    grad_normed1_own = send_home(grad_normed1_own, own, seqs, n_head, n_seq)
    grad_qkv_weight, grad_proj_weight, grad_router, grad_ffn_gain, grad_attn_gain, grad_bias, grad_table = outputs(
        weights_first, weights_last, small, attn_gain.reshape(chunks, lanes), 3 * head_dim, hidden, n_seq
    )
    grad_qkv_weight = grad_qkv_weight.T
    grad_router_weight = grad_router.T
    grad_ffn_gain, grad_attn_gain = grad_ffn_gain.reshape(width), grad_attn_gain.reshape(width)
    grad_router_bias = grad_bias[0, :experts]
    grad_bias_table = grad_table[0, : heads_here * buckets].reshape(heads_here, buckets).T
    grad_tokens = last_step(
        grad_normed1_own.reshape(rows, width), x_own, grad_mid, attn_gain.reshape(chunks, lanes)
    )
    grad_tokens = jnp.moveaxis(grad_tokens.reshape(own, tsd, width), 0, 1)
    return (
        output,
        grad_tokens,
        grad_attn_gain,
        grad_qkv_weight,
        grad_bias_table,
        grad_proj_weight,
        grad_ffn_gain,
        grad_router_weight,
        grad_router_bias,
        grad_expert_in,
        grad_expert_out,
    )


def solution(mesh):
    placed = (
        P("seq", None, None),
        P(),
        P(None, "head"),
        P(None, "head"),
        P("head", None),
        P(),
        P(),
        P(),
        P(("head", "seq"), None, None),
        P(("head", "seq"), None, None),
        P(),
        P("seq", "head"),
        P("seq", "head"),
        P("seq", "head", None),
    )
    return jax.shard_map(
        functools.partial(local, mesh.shape["head"], mesh.shape["seq"]),
        mesh=mesh,
        in_specs=placed,
        out_specs=(
            P("seq", "head", None),
            P("seq", "head", None),
            P(),
            P(None, "head"),
            P(None, "head"),
            P("head", None),
            P(),
            P(),
            P(),
            P(("head", "seq"), None, None),
            P(("head", "seq"), None, None),
        ),
        check_vma=False,
    )
```
